32 devices in a mesh: gx: 8 (over z, y), gy: 2 (over x), gz: 2 (over core).
Axes of the slice: x: 2, y: 2, z: 4, core: 2. Of those that a mesh axis runs over, the one named last changes fastest.
Arguments:
- dual_result_fields: float32 [5, 64, 32, 512], P(None, 'gx', 'gy', 'gz'), may hold values from -24 to 24, as said below
- scaled_mass_per_volume: float32 [64, 32, 512], P('gx', 'gy', 'gz'), may hold values from 0.2 to 2.5
- scaled_thermal_level: float32 [64, 32, 512], P('gx', 'gy', 'gz'), may hold values from 0.6 to 2
- interaction_matrix: float32 [5, 5], replicated, may hold values from -2 to 2
Outputs:
- adjoint_prior: float32 [5, 64, 32, 512], P(None, 'gx', 'gy', 'gz')
The draws below stay inside these ranges and needn't reach their ends.
Inputs may be any that keep to these rules, and one draw needn't show every extreme that they name: `dual_result_fields`: finite values.
All inputs are finite; a program needn't handle non-finite values.
Results may differ from the reference program's by a relative error of at most 0.00026.
Values sent between devices are 32-bit elements; how exact they have to be, the bound alone decides.
A program may use at most 64 MiB of HBM per device.

```python
import jax
import jax.numpy as jnp
from jax import lax

FIELDS = 5
FLOWWARD_COUNT = 64
TRANSVERSE_CELLS = 32
LATERAL_COUNT = 512


def draw_dual_result_fields(key, part):
    key = jax.random.fold_in(key, 7)
    return jnp.clip(4.0 * jax.random.normal(key, (FIELDS, FLOWWARD_COUNT, TRANSVERSE_CELLS, LATERAL_COUNT), jnp.float32), -24.0, 24.0)


def block_levels(own_key, extent, split, least, top_value):
    factor_of = 1.0
    for dim, blocks in split:
        draws = jax.random.uniform(jax.random.fold_in(jax.random.fold_in(own_key, 6), dim), (blocks,), jnp.float32, least / len(split), top_value / len(split))
        factor_of = factor_of * jnp.repeat(jnp.exp(draws), extent[dim] // blocks).reshape((-1,) + (1,) * (len(extent) - 1 - dim))
    return factor_of


def gaussian(own_key, shape, scale, bound, kind=jnp.bfloat16):
    return jnp.clip(scale * jax.random.normal(own_key, shape, jnp.float32), -bound, bound).astype(kind)


def setup_inputs(seed: int = 0) -> dict:
    splits = jax.random.split(jax.random.key(seed), 5)
    return {
        "dual_result_fields": draw_dual_result_fields(jax.random.fold_in(splits[4], 71), 0),
        "scaled_mass_per_volume": jnp.clip(0.2 + 2.3 * jax.random.uniform(splits[1], (FLOWWARD_COUNT, TRANSVERSE_CELLS, LATERAL_COUNT), jnp.float32) ** block_levels(splits[1], (FLOWWARD_COUNT, TRANSVERSE_CELLS, LATERAL_COUNT), ((0, 8), (1, 2), (2, 2)), -0.2, 0.2), 0.2, 2.5),
        "scaled_thermal_level": jnp.clip(0.6 + 1.4 * jax.random.uniform(splits[2], (FLOWWARD_COUNT, TRANSVERSE_CELLS, LATERAL_COUNT), jnp.float32) ** block_levels(splits[2], (FLOWWARD_COUNT, TRANSVERSE_CELLS, LATERAL_COUNT), ((0, 8), (1, 2), (2, 2)), -0.2, 0.2), 0.6, 2.0),
        "interaction_matrix": gaussian(splits[3], (FIELDS, FIELDS), 0.45, 2.0, jnp.float32),
    }


def central(padded, axis, length):

    def shifted(offset):
        return lax.slice_in_dim(padded, 3 + offset, 3 + offset + length, axis=axis)
    return 0.75 * (shifted(1) - shifted(-1)) - 0.15 * (shifted(2) - shifted(-2)) + (shifted(3) - shifted(-3)) / 60.0

def pressure_wave_celerity(scaled_mass_per_volume, scaled_thermal_level):
    cohesion_pressure_part = 1.5 * (1.0 + 0.392 * (1.0 - jnp.sqrt(scaled_thermal_level))) ** 2
    divisor_quantity = 1.0 + 0.5 * scaled_mass_per_volume - 0.0625 * scaled_mass_per_volume * scaled_mass_per_volume
    return scaled_thermal_level / (1.0 - 0.25 * scaled_mass_per_volume) ** 2 - cohesion_pressure_part * (2.0 * scaled_mass_per_volume * divisor_quantity - scaled_mass_per_volume * scaled_mass_per_volume * (0.5 - 0.125 * scaled_mass_per_volume)) / (divisor_quantity * divisor_quantity)

def reference(dual_result_fields, scaled_mass_per_volume, scaled_thermal_level, interaction_matrix):
    length = dual_result_fields.shape[1]
    stiffness = length * length / 4.0
    modes = jnp.arange(length // 2 + 1).astype(dual_result_fields.dtype)
    eigen_values = 1.0 + 2.0 * stiffness * (1.0 - jnp.cos(2.0 * jnp.pi * modes / length))

    def solve_field(one_field):
        spectrum = jnp.fft.rfft(one_field, axis=0)
        return jnp.fft.irfft(spectrum / eigen_values[:, None, None], n=length, axis=0).astype(one_field.dtype)
    implicit = lax.map(solve_field, dual_result_fields)

    def slope_field(one_field):
        along_y = central(jnp.pad(one_field, ((0, 0), (3, 3), (0, 0))), 1, one_field.shape[1])
        along_z = central(jnp.pad(one_field, ((0, 0), (0, 0), (3, 3)), mode='wrap'), 2, one_field.shape[2])
        return along_y + along_z
    slopes = lax.map(slope_field, implicit)
    wave_celerity_factor = pressure_wave_celerity(scaled_mass_per_volume, scaled_thermal_level)
    coupled = jnp.einsum('kj,kxyz->jxyz', interaction_matrix, slopes, precision=lax.Precision.HIGHEST)
    return implicit + wave_celerity_factor[None] * coupled
```

```python
import functools
import math

import jax
import jax.numpy as jnp
from jax import lax
from jax.experimental import pallas as pl
from jax.experimental.pallas import tpu as pltpu
from jax.sharding import PartitionSpec as P

MESH = pl.DeviceIdType.MESH
PIECES = 8
HALO = 8


def line_constants(total_cells):
    stiffness = total_cells * total_cells / 4.0
    half = 1.0 + 0.5 / stiffness
    decay = half - math.sqrt(half**2 - 1.0)
    return decay, decay / (stiffness * (1.0 - decay * decay))


def remote(src, dst, send_sem, recv_sem, target):
    return pltpu.make_async_remote_copy(
        src_ref=src, dst_ref=dst, send_sem=send_sem, recv_sem=recv_sem,
        device_id=target, device_id_type=MESH,
    )


def edges(block):
    width = block.shape[-1] // 2
    lane = lax.broadcasted_iota(jnp.int32, block.shape[:-1] + (width,), block.ndim - 1)
    return jnp.where(lane < width // 2, block[..., :width], block[..., width:])


def exchange_kernel(
    count_x, count_y, decay,
    a_ref, pq, pq_low, pq_high, pq_z, a_low, a_high, a_z,
    a_v, ends, own_in, own_out, pq_edges, a_edges,
    load_sem, send1, recv1, send2, recv2, send_a, recv_a, send_p, recv_p,
):
    fields, length, rows, lanes = a_v.shape
    stride = count_x // PIECES
    my_x, my_y, my_z = (lax.axis_index(name) for name in ("gx", "gy", "gz"))
    has_low, has_high = my_y > 0, my_y < count_y - 1
    low, high, other = {"gy": my_y - 1}, {"gy": my_y + 1}, {"gz": 1 - my_z}

    load = pltpu.make_async_copy(a_ref, a_v, load_sem)
    load.start()

    barrier = pltpu.get_barrier_semaphore()
    for step in range(1, count_x):
        peer = lax.rem(my_x + step, count_x)
        pl.semaphore_signal(barrier, inc=1, device_id={"gx": peer}, device_id_type=MESH)
    pl.semaphore_signal(barrier, inc=1, device_id=other, device_id_type=MESH)

    @pl.when(has_low)
    def _():
        pl.semaphore_signal(barrier, inc=1, device_id=low, device_id_type=MESH)

    @pl.when(has_high)
    def _():
        pl.semaphore_signal(barrier, inc=1, device_id=high, device_id_type=MESH)

    load.wait()
    upward = a_v[:, 0]
    downward = a_v[:, length - 1]
    for i in range(1, length):
        upward = a_v[:, i] + decay * upward
        downward = a_v[:, length - 1 - i] + decay * downward
    for yh in range(2):
        for kind in range(2):
            for zh in range(2):
                value = (upward, downward)[kind]
                ends[yh * 4 + kind * 2 + zh] = value[
                    :, yh * 8 : yh * 8 + 8, zh * (lanes // 2) : (zh + 1) * (lanes // 2)
                ]

    neighbours = has_low.astype(jnp.int32) + has_high.astype(jnp.int32)
    pl.semaphore_wait(barrier, count_x + neighbours)

    my_piece = my_x // stride
    owner = lax.rem(my_x, stride) == 0

    def end_copy(step):
        piece = lax.rem(my_piece + step, PIECES)
        target = piece * stride
        return target, remote(
            ends.at[piece], own_in.at[my_x], send1.at[step], recv1.at[my_x], {"gx": target}
        )

    for step in range(PIECES):
        if step == 0 and stride == 1:
            own_in[my_x] = ends[my_piece]
            continue
        target, copy = end_copy(step)

        @pl.when(target != my_x)
        def _():
            copy.start()

        if step == 0:

            @pl.when(target == my_x)
            def _():
                own_in[my_x] = ends[my_piece]

    a_edges[...] = edges(a_v[...])
    copy_az = remote(a_edges, a_z, send_a.at[0], recv_a.at[0], other)
    copy_az.start()
    copy_alow = remote(a_v.at[:, :, 0:HALO, :], a_high, send_a.at[1], recv_a.at[1], low)
    copy_ahigh = remote(
        a_v.at[:, :, rows - HALO : rows, :], a_low, send_a.at[2], recv_a.at[2], high
    )

    @pl.when(has_low)
    def _():
        copy_alow.start()

    @pl.when(has_high)
    def _():
        copy_ahigh.start()

    kind = lax.rem(my_piece // 2, 2)

    def result_copy(position, device):
        return remote(
            own_out.at[device], pq.at[my_piece], send2.at[device], recv2.at[my_piece],
            {"gx": device},
        )

    def own():
        for device in range(count_x):

            @pl.when(device != my_x)
            def _():
                remote(
                    own_in.at[device], own_in.at[device], send1.at[0], recv1.at[device],
                    {"gx": device},
                ).wait_recv()

        def index(position):
            return jnp.where(kind == 1, count_x - 1 - position, position)

        power = decay**length
        total = own_in[index(0)]
        for position in range(1, count_x):
            total = own_in[index(position)] + power * total
        total = total / (1.0 - power**count_x)
        for position in range(count_x):
            device = index(position)
            own_out[device] = total
            if position < count_x - 1:
                total = own_in[device] + power * total

            @pl.when(device != my_x)
            def _():
                result_copy(position, device).start()

            @pl.when(device == my_x)
            def _():
                pq[my_piece] = own_out[my_x]

    if stride == 1:
        own()
    else:
        pl.when(owner)(own)

    for piece in range(PIECES):

        @pl.when(piece * stride != my_x)
        def _():
            remote(
                own_out.at[0], pq.at[piece], send2.at[0], recv2.at[piece],
                {"gx": piece * stride},
            ).wait_recv()

    copy_plow = remote(pq.at[0:4], pq_high, send_p.at[1], recv_p.at[1], low)
    copy_phigh = remote(pq.at[4:8], pq_low, send_p.at[2], recv_p.at[2], high)

    @pl.when(has_low)
    def _():
        copy_plow.start()

    @pl.when(has_high)
    def _():
        copy_phigh.start()

    lane = lax.broadcasted_iota(jnp.int32, (fields, 8, lanes // 2), 2)
    for pair in range(4):
        pq_edges[pair] = jnp.where(lane < lanes // 4, pq[2 * pair], pq[2 * pair + 1])
    copy_pz = remote(pq_edges, pq_z, send_p.at[0], recv_p.at[0], other)
    copy_pz.start()

    copy_az.wait()
    copy_pz.wait()

    @pl.when(has_low)
    def _():
        copy_alow.wait_send()
        copy_plow.wait_send()
        copy_ahigh.wait_recv()
        copy_phigh.wait_recv()

    @pl.when(has_high)
    def _():
        copy_ahigh.wait_send()
        copy_phigh.wait_send()
        copy_alow.wait_recv()
        copy_plow.wait_recv()

    @pl.when(jnp.logical_not(has_low))
    def _():
        a_low[...] = jnp.zeros_like(a_low)
        pq_low[...] = jnp.zeros_like(pq_low)

    @pl.when(jnp.logical_not(has_high))
    def _():
        a_high[...] = jnp.zeros_like(a_high)
        pq_high[...] = jnp.zeros_like(pq_high)

    for step in range(PIECES):
        if step == 0 and stride == 1:
            continue
        target, copy = end_copy(step)

        @pl.when(target != my_x)
        def _():
            copy.wait_send()

    def finish():
        for device in range(count_x):

            @pl.when(device != my_x)
            def _():
                result_copy(0, device).wait_send()

    if stride == 1:
        finish()
    else:
        pl.when(owner)(finish)


def exchange(a, count_x, count_y, decay):
    fields, length, rows, lanes = a.shape
    half = lanes // 2
    shape = lambda *sizes: jax.ShapeDtypeStruct(sizes, jnp.float32)
    vmem = pl.BlockSpec(memory_space=pltpu.VMEM)
    dma = pltpu.SemaphoreType.DMA
    outs = [
        shape(PIECES, fields, 8, half), shape(4, fields, 8, half), shape(4, fields, 8, half),
        shape(4, fields, 8, half), shape(fields, length, HALO, lanes),
        shape(fields, length, HALO, lanes), shape(fields, length, rows, half),
    ]
    return pl.pallas_call(
        functools.partial(exchange_kernel, count_x, count_y, decay),
        out_shape=outs,
        in_specs=[pl.BlockSpec(memory_space=pl.ANY)],
        out_specs=[vmem] * len(outs),
        scratch_shapes=[
            pltpu.VMEM((fields, length, rows, lanes), jnp.float32),
            pltpu.VMEM((PIECES, fields, 8, half), jnp.float32),
            pltpu.VMEM((count_x, fields, 8, half), jnp.float32),
            pltpu.VMEM((count_x, fields, 8, half), jnp.float32),
            pltpu.VMEM((4, fields, 8, half), jnp.float32),
            pltpu.VMEM((fields, length, rows, half), jnp.float32),
            dma, dma((PIECES,)), dma((count_x,)), dma((count_x,)), dma((PIECES,)),
            dma((3,)), dma((3,)), dma((3,)), dma((3,)),
        ],
        compiler_params=pltpu.CompilerParams(
            collective_id=0, has_side_effects=True, vmem_limit_bytes=24 * 2**20
        ),
    )(a)


def pressure_wave_celerity(mass, level):
    attraction = 1.5 * (1.0 + 0.392 * (1.0 - jnp.sqrt(level))) ** 2
    q = 1.0 + 0.5 * mass - 0.0625 * mass * mass
    return level / (1.0 - 0.25 * mass) ** 2 - attraction * (
        2.0 * mass * q - mass * mass * (0.5 - 0.125 * mass)
    ) / (q * q)


def solved(block, up, down, decay, scale):
    length = len(block)
    upward, downward = [None] * length, [None] * length
    for i in range(length):
        up = block[i] + decay * up
        upward[i] = up
    for i in range(length - 1, -1, -1):
        down = decay * down
        downward[i] = down
        down = block[i] + down
    return [scale * (upward[i] + downward[i]) for i in range(length)]


def finish_kernel(
    decay, scale,
    m_ref, a, mass, level, pq, pq_low, pq_high, pq_z, a_low, a_high, a_z, out, ext, edge,
):
    fields, length, rows, lanes = a.shape

    def pair(ref, piece, f):
        return jnp.concatenate([ref[piece, f], ref[piece + 1, f]], axis=1)

    for f in range(fields):
        for block, values, at in (
            (a_low, (pair(pq_low, 0, f), pair(pq_low, 2, f)), 0),
            (a, (pair(pq, 0, f), pair(pq, 2, f)), HALO),
            (a, (pair(pq, 4, f), pair(pq, 6, f)), HALO + 8),
            (a_high, (pair(pq_high, 0, f), pair(pq_high, 2, f)), HALO + rows),
        ):
            start = at - HALO if block is a else 0
            cells = [block[f, i, start : start + 8, :] for i in range(length)]
            for i, value in enumerate(solved(cells, *values, decay, scale)):
                ext[f, i, at : at + 8, :] = value
        for yh in range(2):
            cells = [a_z[f, i, yh * 8 : yh * 8 + 8, :] for i in range(length)]
            values = (pq_z[yh * 2, f], pq_z[yh * 2 + 1, f])
            for i, value in enumerate(solved(cells, *values, decay, scale)):
                edge[f, i, yh * 8 : yh * 8 + 8, :] = value

    def plane(i, carry):
        celerity = pressure_wave_celerity(mass[i], level[i])
        slopes, centres = [], []
        for f in range(fields):
            at = lambda o: ext[f, i, HALO + o : HALO + o + rows, :]
            centre = at(0)
            ring = jnp.concatenate([centre, edge[f, i]], axis=1)
            turn = lambda o: pltpu.roll(ring, (-o) % ring.shape[1], 1)[:, :lanes]
            slopes.append(
                0.75 * ((at(1) - at(-1)) + (turn(1) - turn(-1)))
                - 0.15 * ((at(2) - at(-2)) + (turn(2) - turn(-2)))
                + ((at(3) - at(-3)) + (turn(3) - turn(-3))) * (1.0 / 60.0)
            )
            centres.append(centre)
        for j in range(fields):
            coupled = m_ref[0, j] * slopes[0]
            for k in range(1, fields):
                coupled = coupled + m_ref[k, j] * slopes[k]
            out[j, i] = centres[j] + celerity * coupled
        return carry

    lax.fori_loop(0, length, plane, 0)


def finish(m, a, mass, level, arrived, decay, scale):
    fields, length, rows, lanes = a.shape
    vmem = pl.BlockSpec(memory_space=pltpu.VMEM)
    return pl.pallas_call(
        functools.partial(finish_kernel, decay, scale),
        out_shape=jax.ShapeDtypeStruct(a.shape, jnp.float32),
        in_specs=[pl.BlockSpec(memory_space=pltpu.SMEM)] + [vmem] * (3 + len(arrived)),
        out_specs=vmem,
        scratch_shapes=[
            pltpu.VMEM((fields, length, rows + 2 * HALO, lanes), jnp.float32),
            pltpu.VMEM((fields, length, rows, lanes // 2), jnp.float32),
        ],
        compiler_params=pltpu.CompilerParams(vmem_limit_bytes=24 * 2**20),
    )(m, a, mass, level, *arrived)


def solution(mesh):
    count_x, count_y = mesh.shape["gx"], mesh.shape["gy"]

    def per_device(a, mass, level, m):
        decay, scale = line_constants(a.shape[1] * count_x)
        arrived = exchange(a, count_x, count_y, decay)
        return finish(m, a, mass, level, arrived, decay, scale)

    in_specs = (P(None, "gx", "gy", "gz"), P("gx", "gy", "gz"), P("gx", "gy", "gz"), P())
    out_specs = P(None, "gx", "gy", "gz")
    return jax.shard_map(
        per_device, mesh=mesh, in_specs=in_specs, out_specs=out_specs, check_vma=False
    )
```

```python
import functools
import math

import jax
import jax.numpy as jnp
from jax import lax
from jax.experimental import pallas as pl
from jax.experimental.pallas import tpu as pltpu
from jax.sharding import PartitionSpec as P

MESH = pl.DeviceIdType.MESH
PIECES = 8
HALO = 8
STEPS = (4, 3, 5, 2, 6, 1, 7)


def line_constants(total_cells):
    stiffness = total_cells * total_cells / 4.0
    half = 1.0 + 0.5 / stiffness
    decay = half - math.sqrt(half**2 - 1.0)
    return decay, decay / (stiffness * (1.0 - decay * decay))


def remote(src, dst, send_sem, recv_sem, target):
    return pltpu.make_async_remote_copy(
        src_ref=src, dst_ref=dst, send_sem=send_sem, recv_sem=recv_sem,
        device_id=target, device_id_type=MESH,
    )


def edges(first, second):
    lane = lax.broadcasted_iota(jnp.int32, first.shape, first.ndim - 1)
    return jnp.where(lane < first.shape[-1] // 2, first, second)


def packed(first, second, low):
    row = lax.broadcasted_iota(jnp.int32, first.shape, first.ndim - 2)
    return jnp.where((row < 4) == low, first, pltpu.roll(second, 4, first.ndim - 2))


def slope(ext, edge, at_index, rows, lanes):
    at = lambda o: ext[(*at_index, slice(HALO + o, HALO + o + rows), slice(None))]
    ring = jnp.concatenate([at(0), edge[at_index]], axis=1)
    turn = lambda o: pltpu.roll(ring, (-o) % ring.shape[1], 1)[:, :lanes]
    return (
        0.75 * ((at(1) - at(-1)) + (turn(1) - turn(-1)))
        - 0.15 * ((at(2) - at(-2)) + (turn(2) - turn(-2)))
        + ((at(3) - at(-3)) + (turn(3) - turn(-3))) * (1.0 / 60.0)
    )


def exchange_kernel(
    count_x, count_y, decay, scale,
    a_ref, mass_ref, level_ref, m_ref, base, celerity, entering,
    a_v, mass, level, m, ends, own_in, own_out, pq, ext, u_edges, u_z, u_to_low, u_to_high,
    u_low, u_high, pq_ext, pq_edges, pq_z, p_to_low, p_to_high, p_low, p_high,
    load_sem, send1, recv1, send2, recv2, send_u, recv_u, send_p, recv_p,
):
    fields, length, rows, lanes = a_v.shape
    half = lanes // 2
    stride = count_x // PIECES
    my_x, my_y, my_z = (lax.axis_index(name) for name in ("gx", "gy", "gz"))
    has_low, has_high = my_y > 0, my_y < count_y - 1
    low, high, other = {"gy": my_y - 1}, {"gy": my_y + 1}, {"gz": 1 - my_z}

    load = pltpu.make_async_copy(a_ref, a_v, load_sem.at[0])
    load.start()
    later = [
        pltpu.make_async_copy(source, target, load_sem.at[1 + k])
        for k, (source, target) in enumerate(
            ((mass_ref, mass), (level_ref, level), (m_ref, m))
        )
    ]

    barrier = pltpu.get_barrier_semaphore()
    for step in range(1, count_x):
        peer = lax.rem(my_x + step, count_x)
        pl.semaphore_signal(barrier, inc=1, device_id={"gx": peer}, device_id_type=MESH)
    pl.semaphore_signal(barrier, inc=1, device_id=other, device_id_type=MESH)

    @pl.when(has_low)
    def _():
        pl.semaphore_signal(barrier, inc=1, device_id=low, device_id_type=MESH)

    @pl.when(has_high)
    def _():
        pl.semaphore_signal(barrier, inc=1, device_id=high, device_id_type=MESH)

    for copy in later:
        copy.start()

    load.wait()

    def field_ends(f, carry):
        upward = a_v[f, 0]
        downward = a_v[f, length - 1]
        for i in range(1, length):
            upward = a_v[f, i] + decay * upward
            downward = a_v[f, length - 1 - i] + decay * downward
        for yh in range(2):
            for kind in range(2):
                value = scale * (upward, downward)[kind][yh * 8 : yh * 8 + 8, :]
                for zh in range(2):
                    ends[yh * 4 + kind * 2 + zh, f] = value[:, zh * half : (zh + 1) * half]
        return carry

    lax.fori_loop(0, fields, field_ends, 0)

    neighbours = has_low.astype(jnp.int32) + has_high.astype(jnp.int32)
    pl.semaphore_wait(barrier, count_x + neighbours)

    my_piece = my_x // stride
    owner = lax.rem(my_x, stride) == 0
    steps = STEPS if stride == 1 else STEPS + (0,)

    def end_copy(step):
        piece = lax.rem(my_piece + step, PIECES)
        target = piece * stride
        return target, remote(
            ends.at[piece], own_in.at[my_x], send1.at[step], recv1.at[my_x], {"gx": target}
        )

    for step in steps:
        target, copy = end_copy(step)
        if stride == 1:
            copy.start()
        else:
            pl.when(target != my_x)(copy.start)
    if stride == 1:
        own_in[my_x] = ends[my_piece]
    else:

        @pl.when(owner)
        def _():
            own_in[my_x] = ends[my_piece]

    def field_solve(f, carry):
        upward = [a_v[f, 0]]
        for i in range(1, length):
            upward.append(a_v[f, i] + decay * upward[-1])
        down = jnp.zeros_like(upward[0])
        for i in range(length - 1, -1, -1):
            value = scale * (upward[i] + decay * down)
            down = a_v[f, i] + decay * down
            ext[f, i, HALO : HALO + rows, :] = value
            u_edges[f, i] = edges(value[:, :half], value[:, half:])
        for t in range(length // 2):
            u_to_low[f, t] = packed(
                ext[f, 2 * t, HALO : HALO + 8, :], ext[f, 2 * t + 1, HALO : HALO + 8, :], True
            )
            u_to_high[f, t] = packed(
                ext[f, 2 * t, HALO + rows - 8 : HALO + rows, :],
                ext[f, 2 * t + 1, HALO + rows - 8 : HALO + rows, :],
                False,
            )
        return carry

    lax.fori_loop(0, fields, field_solve, 0)
    copy_uz = remote(u_edges, u_z, send_u.at[0], recv_u.at[0], other)
    copy_uz.start()
    copy_ulow = remote(u_to_low, u_high, send_u.at[1], recv_u.at[1], low)
    copy_uhigh = remote(u_to_high, u_low, send_u.at[2], recv_u.at[2], high)
    pl.when(has_low)(copy_ulow.start)
    pl.when(has_high)(copy_uhigh.start)

    @pl.when(jnp.logical_not(has_low))
    def _():
        u_low[...] = jnp.zeros_like(u_low)
        p_low[...] = jnp.zeros_like(p_low)

    @pl.when(jnp.logical_not(has_high))
    def _():
        u_high[...] = jnp.zeros_like(u_high)
        p_high[...] = jnp.zeros_like(p_high)

    kind = lax.rem(my_piece // 2, 2)

    def result_copy(step):
        device = lax.rem(my_x + step, count_x)
        return remote(
            own_out.at[device], pq.at[my_piece], send2.at[step], recv2.at[my_piece],
            {"gx": device},
        )

    def own():
        for step in range(1, count_x):
            device = lax.rem(my_x + step, count_x)
            remote(
                own_in.at[device], own_in.at[device], send1.at[0], recv1.at[device],
                {"gx": device},
            ).wait_recv()

        def index(position):
            return jnp.where(kind == 1, count_x - 1 - position, position)

        power = decay**length
        total = own_in[index(0)]
        for position in range(1, count_x):
            total = own_in[index(position)] + power * total
        total = total * (1.0 / (1.0 - power**count_x))
        for position in range(count_x):
            device = index(position)
            own_out[device] = total
            if position < count_x - 1:
                total = own_in[device] + power * total
        for step in far_first:
            result_copy(step).start()
        pq[my_piece] = own_out[my_x]

    far_first = sorted(range(1, count_x), key=lambda step: abs(2 * step - count_x))
    if stride == 1:
        own()
    else:
        pl.when(owner)(own)

    copy_uz.wait_recv()
    pl.when(has_low)(copy_uhigh.wait_recv)
    pl.when(has_high)(copy_ulow.wait_recv)
    for copy in later:
        copy.wait()

    def field_halos(f, carry):
        for t in range(length // 2):
            ext[f, 2 * t, :HALO, :] = u_low[f, t]
            ext[f, 2 * t + 1, :HALO, :] = pltpu.roll(u_low[f, t], 4, 0)
            ext[f, 2 * t, HALO + rows :, :] = u_high[f, t]
            ext[f, 2 * t + 1, HALO + rows :, :] = pltpu.roll(u_high[f, t], 4, 0)
        return carry

    lax.fori_loop(0, fields, field_halos, 0)

    def couple(slopes, j):
        coupled = m[0, j] * slopes[0]
        for k in range(1, fields):
            coupled = coupled + m[k, j] * slopes[k]
        return coupled

    def plane(i, carry):
        speed = pressure_wave_celerity(mass[i], level[i])
        celerity[i] = speed
        slopes = [slope(ext, u_z, (f, i), rows, lanes) for f in range(fields)]
        for j in range(fields):
            base[j, i] = ext[j, i, HALO : HALO + rows, :] + speed * couple(slopes, j)
        return carry

    lax.fori_loop(0, length, plane, 0)

    for piece in range(PIECES):
        arrived = remote(
            own_out.at[0], pq.at[piece], send2.at[0], recv2.at[piece], {"gx": piece * stride}
        )
        pl.when(piece * stride != my_x)(arrived.wait_recv)

    for zh in range(2):
        p_to_low[zh] = packed(pq[zh], pq[2 + zh], True)
        p_to_high[zh] = packed(pq[4 + zh], pq[6 + zh], False)
    copy_plow = remote(p_to_low, p_high, send_p.at[1], recv_p.at[1], low)
    copy_phigh = remote(p_to_high, p_low, send_p.at[2], recv_p.at[2], high)
    pl.when(has_low)(copy_plow.start)
    pl.when(has_high)(copy_phigh.start)
    for kd in range(2):
        for yh in range(2):
            piece = yh * 4 + kd * 2
            pq_edges[kd, :, yh * 8 : yh * 8 + 8, :] = edges(pq[piece], pq[piece + 1])
            for zh in range(2):
                pq_ext[
                    kd, :, HALO + yh * 8 : HALO + yh * 8 + 8, zh * half : (zh + 1) * half
                ] = pq[piece + zh]
    copy_pz = remote(pq_edges, pq_z, send_p.at[0], recv_p.at[0], other)
    copy_pz.start()
    entering[0:2] = pq_ext[:, :, HALO : HALO + rows, :]

    for step in steps:
        target, copy = end_copy(step)
        if stride == 1:
            copy.wait_send()
        else:
            pl.when(target != my_x)(copy.wait_send)
    copy_uz.wait_send()
    pl.when(has_low)(copy_ulow.wait_send)
    pl.when(has_high)(copy_uhigh.wait_send)

    def sent():
        for step in far_first:
            result_copy(step).wait_send()

    if stride == 1:
        sent()
    else:
        pl.when(owner)(sent)

    copy_pz.wait()
    pl.when(has_low)(copy_plow.wait_send)
    pl.when(has_high)(copy_phigh.wait_send)
    pl.when(has_low)(copy_phigh.wait_recv)
    pl.when(has_high)(copy_plow.wait_recv)

    for zh in range(2):
        columns = slice(zh * half, (zh + 1) * half)
        pq_ext[0, :, :HALO, columns] = p_low[zh]
        pq_ext[1, :, :HALO, columns] = pltpu.roll(p_low[zh], 4, 1)
        pq_ext[0, :, HALO + rows :, columns] = p_high[zh]
        pq_ext[1, :, HALO + rows :, columns] = pltpu.roll(p_high[zh], 4, 1)
    for kd in range(2):
        slopes = [slope(pq_ext, pq_z, (kd, f), rows, lanes) for f in range(fields)]
        for j in range(fields):
            entering[2 + kd, j] = couple(slopes, j)


def exchange(a, mass, level, m, count_x, count_y, decay, scale):
    fields, length, rows, lanes = a.shape
    half = lanes // 2
    vmem = pl.BlockSpec(memory_space=pltpu.VMEM)
    hbm = pl.BlockSpec(memory_space=pltpu.HBM)
    dma = pltpu.SemaphoreType.DMA
    buffer = lambda *sizes: pltpu.VMEM(sizes, jnp.float32)
    shape = lambda *sizes: jax.ShapeDtypeStruct(sizes, jnp.float32)
    return pl.pallas_call(
        functools.partial(exchange_kernel, count_x, count_y, decay, scale),
        out_shape=[
            shape(*a.shape), shape(length, rows, lanes), shape(4, fields, rows, lanes)
        ],
        in_specs=[hbm] * 4,
        out_specs=[vmem] * 3,
        scratch_shapes=[
            buffer(*a.shape), buffer(length, rows, lanes), buffer(length, rows, lanes),
            pltpu.SMEM((fields, fields), jnp.float32),
            buffer(PIECES, fields, 8, half),
            buffer(count_x, fields, 8, half),
            buffer(count_x, fields, 8, half),
            buffer(PIECES, fields, 8, half),
            buffer(fields, length, rows + 2 * HALO, lanes),
            buffer(fields, length, rows, half), buffer(fields, length, rows, half),
            buffer(fields, length // 2, 8, lanes), buffer(fields, length // 2, 8, lanes),
            buffer(fields, length // 2, 8, lanes), buffer(fields, length // 2, 8, lanes),
            buffer(2, fields, rows + 2 * HALO, lanes),
            buffer(2, fields, rows, half), buffer(2, fields, rows, half),
            buffer(2, fields, 8, half), buffer(2, fields, 8, half),
            buffer(2, fields, 8, half), buffer(2, fields, 8, half),
            dma((4,)), dma((PIECES,)), dma((count_x,)), dma((count_x,)), dma((PIECES,)),
            dma((3,)), dma((3,)), dma((3,)), dma((3,)),
        ],
        compiler_params=pltpu.CompilerParams(
            collective_id=0, has_side_effects=True, vmem_limit_bytes=24 * 2**20
        ),
    )(a, mass, level, m)


def pressure_wave_celerity(mass, level):
    attraction = 1.5 * (1.0 + 0.392 * (1.0 - jnp.sqrt(level))) ** 2
    q = 1.0 + 0.5 * mass - 0.0625 * mass * mass
    return level / (1.0 - 0.25 * mass) ** 2 - attraction * (
        2.0 * mass * q - mass * mass * (0.5 - 0.125 * mass)
    ) / (q * q)


def finish_kernel(decay, base, celerity, entering, out, result, sems):
    fields, length, rows, lanes = base.shape
    copies = []
    for i in range(length):
        up, down = decay ** (i + 1), decay ** (length - i)
        for j in range(fields):
            straight = up * entering[0, j] + down * entering[1, j]
            coupled = up * entering[2, j] + down * entering[3, j]
            result[j, i] = base[j, i] + straight + celerity[i] * coupled
        copies.append(pltpu.make_async_copy(result.at[:, i], out.at[:, i], sems.at[i]))
        copies[-1].start()
    for copy in copies:
        copy.wait()


def finish(base, celerity, entering, decay):
    vmem = pl.BlockSpec(memory_space=pltpu.VMEM)
    return pl.pallas_call(
        functools.partial(finish_kernel, decay),
        out_shape=jax.ShapeDtypeStruct(base.shape, jnp.float32),
        in_specs=[vmem] * 3,
        out_specs=pl.BlockSpec(memory_space=pltpu.HBM),
        scratch_shapes=[
            pltpu.VMEM(base.shape, jnp.float32), pltpu.SemaphoreType.DMA((base.shape[1],))
        ],
        compiler_params=pltpu.CompilerParams(vmem_limit_bytes=24 * 2**20),
    )(base, celerity, entering)


def solution(mesh):
    count_x, count_y = mesh.shape["gx"], mesh.shape["gy"]

    def per_device(a, mass, level, m):
        decay, scale = line_constants(a.shape[1] * count_x)
        parts = exchange(a, mass, level, m, count_x, count_y, decay, scale)
        return finish(*parts, decay)

    in_specs = (P(None, "gx", "gy", "gz"), P("gx", "gy", "gz"), P("gx", "gy", "gz"), P())
    out_specs = P(None, "gx", "gy", "gz")
    return jax.shard_map(
        per_device, mesh=mesh, in_specs=in_specs, out_specs=out_specs, check_vma=False
    )
```

```python
import functools
import math

import jax
import jax.numpy as jnp
from jax import lax
from jax.experimental import pallas as pl
from jax.experimental.pallas import tpu as pltpu
from jax.sharding import PartitionSpec as P

MESH = pl.DeviceIdType.MESH
PIECES = 8
HALO = 8
STEPS = (4, 3, 5, 2, 6, 1, 7)


def line_constants(total_cells):
    stiffness = total_cells * total_cells / 4.0
    half = 1.0 + 0.5 / stiffness
    decay = half - math.sqrt(half**2 - 1.0)
    return decay, decay / (stiffness * (1.0 - decay * decay))


def remote(src, dst, send_sem, recv_sem, target):
    return pltpu.make_async_remote_copy(
        src_ref=src, dst_ref=dst, send_sem=send_sem, recv_sem=recv_sem,
        device_id=target, device_id_type=MESH,
    )


def edges(first, second):
    lane = lax.broadcasted_iota(jnp.int32, first.shape, first.ndim - 1)
    return jnp.where(lane < first.shape[-1] // 2, first, second)


def packed(first, second, low):
    row = lax.broadcasted_iota(jnp.int32, first.shape, first.ndim - 2)
    return jnp.where((row < 4) == low, first, pltpu.roll(second, 4, first.ndim - 2))


def slope(ext, edge, at_index, rows, lanes):
    at = lambda o: ext[(*at_index, slice(HALO + o, HALO + o + rows), slice(None))]
    ring = jnp.concatenate([at(0), edge[at_index]], axis=1)
    turn = lambda o: pltpu.roll(ring, (-o) % ring.shape[1], 1)[:, :lanes]
    return (
        0.75 * ((at(1) - at(-1)) + (turn(1) - turn(-1)))
        - 0.15 * ((at(2) - at(-2)) + (turn(2) - turn(-2)))
        + ((at(3) - at(-3)) + (turn(3) - turn(-3))) * (1.0 / 60.0)
    )


def exchange_kernel(
    count_x, count_y, decay, scale,
    a_ref, mass_ref, level_ref, m_ref, base, celerity, entering,
    a_v, mass, level, m, ends, own_in, own_out, pq, ext, u_edges, u_z, u_to_low, u_to_high,
    u_low, u_high, pq_ext, pq_edges, pq_z, p_to_low, p_to_high, p_low, p_high,
    load_sem, send1, recv1, send2, recv2, send_u, recv_u, send_p, recv_p,
):
    fields, length, rows, lanes = a_v.shape
    half = lanes // 2
    stride = count_x // PIECES
    my_x, my_y, my_z = (lax.axis_index(name) for name in ("gx", "gy", "gz"))
    has_low, has_high = my_y > 0, my_y < count_y - 1
    low, high, other = {"gy": my_y - 1}, {"gy": my_y + 1}, {"gz": 1 - my_z}

    load = pltpu.make_async_copy(a_ref, a_v, load_sem.at[0])
    load.start()
    later = [
        pltpu.make_async_copy(source, target, load_sem.at[1 + k])
        for k, (source, target) in enumerate(
            ((mass_ref, mass), (level_ref, level), (m_ref, m))
        )
    ]

    barrier = pltpu.get_barrier_semaphore()
    for step in range(1, count_x):
        peer = lax.rem(my_x + step, count_x)
        pl.semaphore_signal(barrier, inc=1, device_id={"gx": peer}, device_id_type=MESH)
    pl.semaphore_signal(barrier, inc=1, device_id=other, device_id_type=MESH)

    @pl.when(has_low)
    def _():
        pl.semaphore_signal(barrier, inc=1, device_id=low, device_id_type=MESH)

    @pl.when(has_high)
    def _():
        pl.semaphore_signal(barrier, inc=1, device_id=high, device_id_type=MESH)

    for copy in later:
        copy.start()

    load.wait()

    def field_ends(f, carry):
        upward = a_v[f, 0]
        downward = a_v[f, length - 1]
        for i in range(1, length):
            upward = a_v[f, i] + decay * upward
            downward = a_v[f, length - 1 - i] + decay * downward
        for yh in range(2):
            for kind in range(2):
                value = scale * (upward, downward)[kind][yh * 8 : yh * 8 + 8, :]
                for zh in range(2):
                    ends[yh * 4 + kind * 2 + zh, f] = value[:, zh * half : (zh + 1) * half]
        return carry

    lax.fori_loop(0, fields, field_ends, 0)

    neighbours = has_low.astype(jnp.int32) + has_high.astype(jnp.int32)
    pl.semaphore_wait(barrier, count_x + neighbours)

    my_piece = my_x // stride
    owner = lax.rem(my_x, stride) == 0
    steps = STEPS if stride == 1 else STEPS + (0,)

    def end_copy(step):
        piece = lax.rem(my_piece + step, PIECES)
        target = piece * stride
        return target, remote(
            ends.at[piece], own_in.at[my_x], send1.at[step], recv1.at[my_x], {"gx": target}
        )

    for step in steps:
        target, copy = end_copy(step)
        if stride == 1:
            copy.start()
        else:
            pl.when(target != my_x)(copy.start)
    if stride == 1:
        own_in[my_x] = ends[my_piece]
    else:

        @pl.when(owner)
        def _():
            own_in[my_x] = ends[my_piece]

    def field_solve(f, carry):
        upward = [a_v[f, 0]]
        for i in range(1, length):
            upward.append(a_v[f, i] + decay * upward[-1])
        down = jnp.zeros_like(upward[0])
        for i in range(length - 1, -1, -1):
            value = scale * (upward[i] + decay * down)
            down = a_v[f, i] + decay * down
            ext[f, i, HALO : HALO + rows, :] = value
            u_edges[f, i] = edges(value[:, :half], value[:, half:])
        for t in range(length // 2):
            u_to_low[f, t] = packed(
                ext[f, 2 * t, HALO : HALO + 8, :], ext[f, 2 * t + 1, HALO : HALO + 8, :], True
            )
            u_to_high[f, t] = packed(
                ext[f, 2 * t, HALO + rows - 8 : HALO + rows, :],
                ext[f, 2 * t + 1, HALO + rows - 8 : HALO + rows, :],
                False,
            )
        return carry

    lax.fori_loop(0, fields, field_solve, 0)
    copy_uz = remote(u_edges, u_z, send_u.at[0], recv_u.at[0], other)
    copy_uz.start()
    copy_ulow = remote(u_to_low, u_high, send_u.at[1], recv_u.at[1], low)
    copy_uhigh = remote(u_to_high, u_low, send_u.at[2], recv_u.at[2], high)
    pl.when(has_low)(copy_ulow.start)
    pl.when(has_high)(copy_uhigh.start)

    @pl.when(jnp.logical_not(has_low))
    def _():
        u_low[...] = jnp.zeros_like(u_low)
        p_low[...] = jnp.zeros_like(p_low)

    @pl.when(jnp.logical_not(has_high))
    def _():
        u_high[...] = jnp.zeros_like(u_high)
        p_high[...] = jnp.zeros_like(p_high)

    kind = lax.rem(my_piece // 2, 2)

    def result_copy(step):
        device = lax.rem(my_x + step, count_x)
        return remote(
            own_out.at[device], pq.at[my_piece], send2.at[step], recv2.at[my_piece],
            {"gx": device},
        )

    def own():
        for step in range(1, count_x):
            device = lax.rem(my_x + step, count_x)
            remote(
                own_in.at[device], own_in.at[device], send1.at[0], recv1.at[device],
                {"gx": device},
            ).wait_recv()

        def index(position):
            return jnp.where(kind == 1, count_x - 1 - position, position)

        power = decay**length
        total = own_in[index(0)]
        for position in range(1, count_x):
            total = own_in[index(position)] + power * total
        total = total * (1.0 / (1.0 - power**count_x))
        for position in range(count_x):
            device = index(position)
            own_out[device] = total
            if position < count_x - 1:
                total = own_in[device] + power * total
        for step in far_first:
            result_copy(step).start()
        pq[my_piece] = own_out[my_x]

    far_first = sorted(range(1, count_x), key=lambda step: abs(2 * step - count_x))
    if stride == 1:
        own()
    else:
        pl.when(owner)(own)

    copy_uz.wait_recv()
    pl.when(has_low)(copy_uhigh.wait_recv)
    pl.when(has_high)(copy_ulow.wait_recv)
    for copy in later:
        copy.wait()

    def field_halos(f, carry):
        for t in range(length // 2):
            ext[f, 2 * t, :HALO, :] = u_low[f, t]
            ext[f, 2 * t + 1, :HALO, :] = pltpu.roll(u_low[f, t], 4, 0)
            ext[f, 2 * t, HALO + rows :, :] = u_high[f, t]
            ext[f, 2 * t + 1, HALO + rows :, :] = pltpu.roll(u_high[f, t], 4, 0)
        return carry

    lax.fori_loop(0, fields, field_halos, 0)

    def couple(slopes, j):
        coupled = m[0, j] * slopes[0]
        for k in range(1, fields):
            coupled = coupled + m[k, j] * slopes[k]
        return coupled

    def plane(i, carry):
        speed = pressure_wave_celerity(mass[i], level[i])
        celerity[i] = speed
        slopes = [slope(ext, u_z, (f, i), rows, lanes) for f in range(fields)]
        for j in range(fields):
            base[j, i] = ext[j, i, HALO : HALO + rows, :] + speed * couple(slopes, j)
        return carry

    lax.fori_loop(0, length, plane, 0)

    for piece in range(PIECES):
        arrived = remote(
            own_out.at[0], pq.at[piece], send2.at[0], recv2.at[piece], {"gx": piece * stride}
        )
        pl.when(piece * stride != my_x)(arrived.wait_recv)

    for zh in range(2):
        p_to_low[zh] = packed(pq[zh], pq[2 + zh], True)
        p_to_high[zh] = packed(pq[4 + zh], pq[6 + zh], False)
    copy_plow = remote(p_to_low, p_high, send_p.at[1], recv_p.at[1], low)
    copy_phigh = remote(p_to_high, p_low, send_p.at[2], recv_p.at[2], high)
    pl.when(has_low)(copy_plow.start)
    pl.when(has_high)(copy_phigh.start)
    for kd in range(2):
        for yh in range(2):
            piece = yh * 4 + kd * 2
            pq_edges[kd, :, yh * 8 : yh * 8 + 8, :] = edges(pq[piece], pq[piece + 1])
            for zh in range(2):
                pq_ext[
                    kd, :, HALO + yh * 8 : HALO + yh * 8 + 8, zh * half : (zh + 1) * half
                ] = pq[piece + zh]
    copy_pz = remote(pq_edges, pq_z, send_p.at[0], recv_p.at[0], other)
    copy_pz.start()
    entering[0:2] = pq_ext[:, :, HALO : HALO + rows, :]

    for step in steps:
        target, copy = end_copy(step)
        if stride == 1:
            copy.wait_send()
        else:
            pl.when(target != my_x)(copy.wait_send)
    copy_uz.wait_send()
    pl.when(has_low)(copy_ulow.wait_send)
    pl.when(has_high)(copy_uhigh.wait_send)

    def sent():
        for step in far_first:
            result_copy(step).wait_send()

    if stride == 1:
        sent()
    else:
        pl.when(owner)(sent)

    copy_pz.wait()
    pl.when(has_low)(copy_plow.wait_send)
    pl.when(has_high)(copy_phigh.wait_send)
    pl.when(has_low)(copy_phigh.wait_recv)
    pl.when(has_high)(copy_plow.wait_recv)

    for zh in range(2):
        columns = slice(zh * half, (zh + 1) * half)
        pq_ext[0, :, :HALO, columns] = p_low[zh]
        pq_ext[1, :, :HALO, columns] = pltpu.roll(p_low[zh], 4, 1)
        pq_ext[0, :, HALO + rows :, columns] = p_high[zh]
        pq_ext[1, :, HALO + rows :, columns] = pltpu.roll(p_high[zh], 4, 1)
    for kd in range(2):
        slopes = [slope(pq_ext, pq_z, (kd, f), rows, lanes) for f in range(fields)]
        for j in range(fields):
            entering[2 + kd, j] = couple(slopes, j)


def exchange(a, mass, level, m, count_x, count_y, decay, scale):
    fields, length, rows, lanes = a.shape
    half = lanes // 2
    vmem = pl.BlockSpec(memory_space=pltpu.VMEM)
    hbm = pl.BlockSpec(memory_space=pltpu.HBM)
    dma = pltpu.SemaphoreType.DMA
    buffer = lambda *sizes: pltpu.VMEM(sizes, jnp.float32)
    shape = lambda *sizes: jax.ShapeDtypeStruct(sizes, jnp.float32)
    return pl.pallas_call(
        functools.partial(exchange_kernel, count_x, count_y, decay, scale),
        out_shape=[
            shape(*a.shape), shape(length, rows, lanes), shape(4, fields, rows, lanes)
        ],
        in_specs=[hbm] * 4,
        out_specs=[vmem] * 3,
        scratch_shapes=[
            buffer(*a.shape), buffer(length, rows, lanes), buffer(length, rows, lanes),
            pltpu.SMEM((fields, fields), jnp.float32),
            buffer(PIECES, fields, 8, half),
            buffer(count_x, fields, 8, half),
            buffer(count_x, fields, 8, half),
            buffer(PIECES, fields, 8, half),
            buffer(fields, length, rows + 2 * HALO, lanes),
            buffer(fields, length, rows, half), buffer(fields, length, rows, half),
            buffer(fields, length // 2, 8, lanes), buffer(fields, length // 2, 8, lanes),
            buffer(fields, length // 2, 8, lanes), buffer(fields, length // 2, 8, lanes),
            buffer(2, fields, rows + 2 * HALO, lanes),
            buffer(2, fields, rows, half), buffer(2, fields, rows, half),
            buffer(2, fields, 8, half), buffer(2, fields, 8, half),
            buffer(2, fields, 8, half), buffer(2, fields, 8, half),
            dma((4,)), dma((PIECES,)), dma((count_x,)), dma((count_x,)), dma((PIECES,)),
            dma((3,)), dma((3,)), dma((3,)), dma((3,)),
        ],
        compiler_params=pltpu.CompilerParams(
            collective_id=0, has_side_effects=True, vmem_limit_bytes=24 * 2**20
        ),
    )(*(pltpu.with_memory_space_constraint(x, pltpu.HBM) for x in (a, mass, level, m)))


def pressure_wave_celerity(mass, level):
    attraction = 1.5 * (1.0 + 0.392 * (1.0 - jnp.sqrt(level))) ** 2
    q = 1.0 + 0.5 * mass - 0.0625 * mass * mass
    return level / (1.0 - 0.25 * mass) ** 2 - attraction * (
        2.0 * mass * q - mass * mass * (0.5 - 0.125 * mass)
    ) / (q * q)


def finish_kernel(decay, base, celerity, entering, out, result, sems):
    fields, length, rows, lanes = base.shape
    copies = []
    for i in range(length):
        up, down = decay ** (i + 1), decay ** (length - i)
        for j in range(fields):
            straight = up * entering[0, j] + down * entering[1, j]
            coupled = up * entering[2, j] + down * entering[3, j]
            result[j, i] = base[j, i] + straight + celerity[i] * coupled
        copies.append(pltpu.make_async_copy(result.at[:, i], out.at[:, i], sems.at[i]))
        copies[-1].start()
    for copy in copies:
        copy.wait()


def finish(base, celerity, entering, decay):
    vmem = pl.BlockSpec(memory_space=pltpu.VMEM)
    return pl.pallas_call(
        functools.partial(finish_kernel, decay),
        out_shape=jax.ShapeDtypeStruct(base.shape, jnp.float32),
        in_specs=[vmem] * 3,
        out_specs=pl.BlockSpec(memory_space=pltpu.HBM),
        scratch_shapes=[
            pltpu.VMEM(base.shape, jnp.float32), pltpu.SemaphoreType.DMA((base.shape[1],))
        ],
        compiler_params=pltpu.CompilerParams(vmem_limit_bytes=24 * 2**20),
    )(base, celerity, entering)


def solution(mesh):
    count_x, count_y = mesh.shape["gx"], mesh.shape["gy"]

    def per_device(a, mass, level, m):
        decay, scale = line_constants(a.shape[1] * count_x)
        parts = exchange(a, mass, level, m, count_x, count_y, decay, scale)
        return finish(*parts, decay)

    in_specs = (P(None, "gx", "gy", "gz"), P("gx", "gy", "gz"), P("gx", "gy", "gz"), P())
    out_specs = P(None, "gx", "gy", "gz")
    return jax.shard_map(
        per_device, mesh=mesh, in_specs=in_specs, out_specs=out_specs, check_vma=False
    )
```

```python
import functools
import math

import jax
import jax.numpy as jnp
from jax import lax
from jax.experimental import pallas as pl
from jax.experimental.pallas import tpu as pltpu
from jax.sharding import PartitionSpec as P

MESH = pl.DeviceIdType.MESH
PIECES = 8
HALO = 8
STEPS = (4, 3, 5, 2, 6, 1, 7)


def line_constants(total_cells):
    stiffness = total_cells * total_cells / 4.0
    half = 1.0 + 0.5 / stiffness
    decay = half - math.sqrt(half**2 - 1.0)
    return decay, decay / (stiffness * (1.0 - decay * decay))


def remote(src, dst, send_sem, recv_sem, target):
    return pltpu.make_async_remote_copy(
        src_ref=src, dst_ref=dst, send_sem=send_sem, recv_sem=recv_sem,
        device_id=target, device_id_type=MESH,
    )


def edges(first, second):
    lane = lax.broadcasted_iota(jnp.int32, first.shape, first.ndim - 1)
    return jnp.where(lane < first.shape[-1] // 2, first, second)


def packed(first, second, low):
    row = lax.broadcasted_iota(jnp.int32, first.shape, first.ndim - 2)
    return jnp.where((row < 4) == low, first, pltpu.roll(second, 4, first.ndim - 2))


def slope(ext, edge, at_index, rows, lanes):
    at = lambda o: ext[(*at_index, slice(HALO + o, HALO + o + rows), slice(None))]
    ring = jnp.concatenate([at(0), edge[at_index]], axis=1)
    turn = lambda o: pltpu.roll(ring, (-o) % ring.shape[1], 1)[:, :lanes]
    return (
        0.75 * ((at(1) - at(-1)) + (turn(1) - turn(-1)))
        - 0.15 * ((at(2) - at(-2)) + (turn(2) - turn(-2)))
        + ((at(3) - at(-3)) + (turn(3) - turn(-3))) * (1.0 / 60.0)
    )


def exchange_kernel(
    count_x, count_y, decay, scale,
    a_ref, mass_ref, level_ref, m_ref, base, celerity, entering,
    a_v, mass, level, m, ends, own_in, own_out, pq, ext, u_edges, u_z, u_to_low, u_to_high,
    u_low, u_high, pq_ext, pq_edges, pq_z, p_to_low, p_to_high, p_low, p_high,
    load_sem, send1, recv1, send2, recv2, send_u, recv_u, send_p, recv_p,
):
    fields, length, rows, lanes = a_v.shape
    half = lanes // 2
    stride = count_x // PIECES
    my_x, my_y, my_z = (lax.axis_index(name) for name in ("gx", "gy", "gz"))
    has_low, has_high = my_y > 0, my_y < count_y - 1
    low, high, other = {"gy": my_y - 1}, {"gy": my_y + 1}, {"gz": 1 - my_z}

    middle = (fields + 1) // 2
    groups = tuple(enumerate((slice(0, middle), slice(middle, fields))))
    loads = [
        pltpu.make_async_copy(a_ref.at[part], a_v.at[part], load_sem.at[g]) for g, part in groups
    ]
    for copy in loads:
        copy.start()
    later = [
        pltpu.make_async_copy(source, target, load_sem.at[2 + k])
        for k, (source, target) in enumerate(
            ((mass_ref, mass), (level_ref, level), (m_ref, m))
        )
    ]

    barrier = pltpu.get_barrier_semaphore()
    for step in range(1, count_x):
        peer = lax.rem(my_x + step, count_x)
        pl.semaphore_signal(barrier, inc=1, device_id={"gx": peer}, device_id_type=MESH)
    pl.semaphore_signal(barrier, inc=1, device_id=other, device_id_type=MESH)

    @pl.when(has_low)
    def _():
        pl.semaphore_signal(barrier, inc=1, device_id=low, device_id_type=MESH)

    @pl.when(has_high)
    def _():
        pl.semaphore_signal(barrier, inc=1, device_id=high, device_id_type=MESH)

    for copy in later:
        copy.start()

    def field_ends(f, carry):
        upward = a_v[f, 0]
        downward = a_v[f, length - 1]
        for i in range(1, length):
            upward = a_v[f, i] + decay * upward
            downward = a_v[f, length - 1 - i] + decay * downward
        for yh in range(2):
            for kind in range(2):
                value = scale * (upward, downward)[kind][yh * 8 : yh * 8 + 8, :]
                for zh in range(2):
                    ends[yh * 4 + kind * 2 + zh, f] = value[:, zh * half : (zh + 1) * half]
        return carry

    my_piece = my_x // stride
    owner = lax.rem(my_x, stride) == 0
    steps = STEPS if stride == 1 else STEPS + (0,)

    def end_copy(group, step):
        g, part = group
        piece = lax.rem(my_piece + step, PIECES)
        target = piece * stride
        return target, remote(
            ends.at[piece, part], own_in.at[my_x, part], send1.at[g, step], recv1.at[g, my_x],
            {"gx": target},
        )

    neighbours = has_low.astype(jnp.int32) + has_high.astype(jnp.int32)
    for g, part in groups:
        loads[g].wait()
        lax.fori_loop(part.start, part.stop, field_ends, 0)
        if g == 0:
            pl.semaphore_wait(barrier, count_x + neighbours)
        for step in steps:
            target, copy = end_copy((g, part), step)
            if stride == 1:
                copy.start()
            else:
                pl.when(target != my_x)(copy.start)
    if stride == 1:
        own_in[my_x] = ends[my_piece]
    else:

        @pl.when(owner)
        def _():
            own_in[my_x] = ends[my_piece]

    def field_solve(f, carry):
        upward = [a_v[f, 0]]
        for i in range(1, length):
            upward.append(a_v[f, i] + decay * upward[-1])
        down = jnp.zeros_like(upward[0])
        for i in range(length - 1, -1, -1):
            value = scale * (upward[i] + decay * down)
            down = a_v[f, i] + decay * down
            ext[f, i, HALO : HALO + rows, :] = value
            u_edges[f, i] = edges(value[:, :half], value[:, half:])
        for t in range(length // 2):
            u_to_low[f, t] = packed(
                ext[f, 2 * t, HALO : HALO + 8, :], ext[f, 2 * t + 1, HALO : HALO + 8, :], True
            )
            u_to_high[f, t] = packed(
                ext[f, 2 * t, HALO + rows - 8 : HALO + rows, :],
                ext[f, 2 * t + 1, HALO + rows - 8 : HALO + rows, :],
                False,
            )
        return carry

    lax.fori_loop(0, fields, field_solve, 0)
    copy_uz = remote(u_edges, u_z, send_u.at[0], recv_u.at[0], other)
    copy_uz.start()
    copy_ulow = remote(u_to_low, u_high, send_u.at[1], recv_u.at[1], low)
    copy_uhigh = remote(u_to_high, u_low, send_u.at[2], recv_u.at[2], high)
    pl.when(has_low)(copy_ulow.start)
    pl.when(has_high)(copy_uhigh.start)

    @pl.when(jnp.logical_not(has_low))
    def _():
        u_low[...] = jnp.zeros_like(u_low)
        p_low[...] = jnp.zeros_like(p_low)

    @pl.when(jnp.logical_not(has_high))
    def _():
        u_high[...] = jnp.zeros_like(u_high)
        p_high[...] = jnp.zeros_like(p_high)

    kind = lax.rem(my_piece // 2, 2)

    def result_copy(group, step):
        g, part = group
        device = lax.rem(my_x + step, count_x)
        return remote(
            own_out.at[device, part], pq.at[my_piece, part], send2.at[g, step],
            recv2.at[g, my_piece], {"gx": device},
        )

    def own(group):
        g, part = group
        for step in range(1, count_x):
            device = lax.rem(my_x + step, count_x)
            remote(
                own_in.at[device, part], own_in.at[device, part], send1.at[g, 0],
                recv1.at[g, device], {"gx": device},
            ).wait_recv()

        def index(position):
            return jnp.where(kind == 1, count_x - 1 - position, position)

        power = decay**length
        total = own_in[index(0), part]
        for position in range(1, count_x):
            total = own_in[index(position), part] + power * total
        total = total * (1.0 / (1.0 - power**count_x))
        for position in range(count_x):
            device = index(position)
            own_out[device, part] = total
            if position < count_x - 1:
                total = own_in[device, part] + power * total
        for step in far_first:
            result_copy(group, step).start()
        pq[my_piece, part] = own_out[my_x, part]

    far_first = sorted(range(1, count_x), key=lambda step: abs(2 * step - count_x))
    for group in groups:
        if stride == 1:
            own(group)
        else:
            pl.when(owner)(functools.partial(own, group))

    copy_uz.wait_recv()
    pl.when(has_low)(copy_uhigh.wait_recv)
    pl.when(has_high)(copy_ulow.wait_recv)
    for copy in later:
        copy.wait()

    def field_halos(f, carry):
        for t in range(length // 2):
            ext[f, 2 * t, :HALO, :] = u_low[f, t]
            ext[f, 2 * t + 1, :HALO, :] = pltpu.roll(u_low[f, t], 4, 0)
            ext[f, 2 * t, HALO + rows :, :] = u_high[f, t]
            ext[f, 2 * t + 1, HALO + rows :, :] = pltpu.roll(u_high[f, t], 4, 0)
        return carry

    lax.fori_loop(0, fields, field_halos, 0)

    def couple(slopes, j):
        coupled = m[0, j] * slopes[0]
        for k in range(1, fields):
            coupled = coupled + m[k, j] * slopes[k]
        return coupled

    def plane(i, carry):
        speed = pressure_wave_celerity(mass[i], level[i])
        celerity[i] = speed
        slopes = [slope(ext, u_z, (f, i), rows, lanes) for f in range(fields)]
        for j in range(fields):
            base[j, i] = ext[j, i, HALO : HALO + rows, :] + speed * couple(slopes, j)
        return carry

    last = []
    for g, part in groups:
        lax.fori_loop(g * length // 2, (g + 1) * length // 2, plane, 0)
        for piece in range(PIECES):
            arrived = remote(
                own_out.at[0, part], pq.at[piece, part], send2.at[g, 0], recv2.at[g, piece],
                {"gx": piece * stride},
            )
            pl.when(piece * stride != my_x)(arrived.wait_recv)
        for zh in range(2):
            p_to_low[zh, part] = packed(pq[zh, part], pq[2 + zh, part], True)
            p_to_high[zh, part] = packed(pq[4 + zh, part], pq[6 + zh, part], False)
        copy_plow = remote(
            p_to_low.at[:, part], p_high.at[:, part], send_p.at[g, 1], recv_p.at[g, 1], low
        )
        copy_phigh = remote(
            p_to_high.at[:, part], p_low.at[:, part], send_p.at[g, 2], recv_p.at[g, 2], high
        )
        pl.when(has_low)(copy_plow.start)
        pl.when(has_high)(copy_phigh.start)
        for kd in range(2):
            for yh in range(2):
                piece = yh * 4 + kd * 2
                pq_edges[kd, part, yh * 8 : yh * 8 + 8, :] = edges(
                    pq[piece, part], pq[piece + 1, part]
                )
        copy_pz = remote(
            pq_edges.at[:, part], pq_z.at[:, part], send_p.at[g, 0], recv_p.at[g, 0], other
        )
        copy_pz.start()
        last.append((copy_pz, copy_plow, copy_phigh))
    for kd in range(2):
        for yh in range(2):
            for zh in range(2):
                pq_ext[
                    kd, :, HALO + yh * 8 : HALO + yh * 8 + 8, zh * half : (zh + 1) * half
                ] = pq[yh * 4 + kd * 2 + zh]
    entering[0:2] = pq_ext[:, :, HALO : HALO + rows, :]

    for group in groups:
        for step in steps:
            target, copy = end_copy(group, step)
            if stride == 1:
                copy.wait_send()
            else:
                pl.when(target != my_x)(copy.wait_send)
    copy_uz.wait_send()
    pl.when(has_low)(copy_ulow.wait_send)
    pl.when(has_high)(copy_uhigh.wait_send)

    def sent():
        for group in groups:
            for step in far_first:
                result_copy(group, step).wait_send()

    if stride == 1:
        sent()
    else:
        pl.when(owner)(sent)

    for copy_pz, copy_plow, copy_phigh in last:
        copy_pz.wait()
        pl.when(has_low)(copy_plow.wait_send)
        pl.when(has_high)(copy_phigh.wait_send)
        pl.when(has_low)(copy_phigh.wait_recv)
        pl.when(has_high)(copy_plow.wait_recv)

    for zh in range(2):
        columns = slice(zh * half, (zh + 1) * half)
        pq_ext[0, :, :HALO, columns] = p_low[zh]
        pq_ext[1, :, :HALO, columns] = pltpu.roll(p_low[zh], 4, 1)
        pq_ext[0, :, HALO + rows :, columns] = p_high[zh]
        pq_ext[1, :, HALO + rows :, columns] = pltpu.roll(p_high[zh], 4, 1)
    for kd in range(2):
        slopes = [slope(pq_ext, pq_z, (kd, f), rows, lanes) for f in range(fields)]
        for j in range(fields):
            entering[2 + kd, j] = couple(slopes, j)


def exchange(a, mass, level, m, count_x, count_y, decay, scale):
    fields, length, rows, lanes = a.shape
    half = lanes // 2
    vmem = pl.BlockSpec(memory_space=pltpu.VMEM)
    hbm = pl.BlockSpec(memory_space=pltpu.HBM)
    dma = pltpu.SemaphoreType.DMA
    buffer = lambda *sizes: pltpu.VMEM(sizes, jnp.float32)
    shape = lambda *sizes: jax.ShapeDtypeStruct(sizes, jnp.float32)
    return pl.pallas_call(
        functools.partial(exchange_kernel, count_x, count_y, decay, scale),
        out_shape=[
            shape(*a.shape), shape(length, rows, lanes), shape(4, fields, rows, lanes)
        ],
        in_specs=[hbm] * 4,
        out_specs=[vmem] * 3,
        scratch_shapes=[
            buffer(*a.shape), buffer(length, rows, lanes), buffer(length, rows, lanes),
            pltpu.SMEM((fields, fields), jnp.float32),
            buffer(PIECES, fields, 8, half),
            buffer(count_x, fields, 8, half),
            buffer(count_x, fields, 8, half),
            buffer(PIECES, fields, 8, half),
            buffer(fields, length, rows + 2 * HALO, lanes),
            buffer(fields, length, rows, half), buffer(fields, length, rows, half),
            buffer(fields, length // 2, 8, lanes), buffer(fields, length // 2, 8, lanes),
            buffer(fields, length // 2, 8, lanes), buffer(fields, length // 2, 8, lanes),
            buffer(2, fields, rows + 2 * HALO, lanes),
            buffer(2, fields, rows, half), buffer(2, fields, rows, half),
            buffer(2, fields, 8, half), buffer(2, fields, 8, half),
            buffer(2, fields, 8, half), buffer(2, fields, 8, half),
            dma((5,)), dma((2, PIECES)), dma((2, count_x)), dma((2, count_x)),
            dma((2, PIECES)), dma((3,)), dma((3,)), dma((2, 3)), dma((2, 3)),
        ],
        compiler_params=pltpu.CompilerParams(
            collective_id=0, has_side_effects=True, vmem_limit_bytes=24 * 2**20
        ),
    )(*(pltpu.with_memory_space_constraint(x, pltpu.HBM) for x in (a, mass, level, m)))


def pressure_wave_celerity(mass, level):
    attraction = 1.5 * (1.0 + 0.392 * (1.0 - jnp.sqrt(level))) ** 2
    q = 1.0 + 0.5 * mass - 0.0625 * mass * mass
    return level / (1.0 - 0.25 * mass) ** 2 - attraction * (
        2.0 * mass * q - mass * mass * (0.5 - 0.125 * mass)
    ) / (q * q)


def finish_kernel(decay, base, celerity, entering, out, result, sems):
    fields, length, rows, lanes = base.shape
    copies = []
    for i in range(length):
        up, down = decay ** (i + 1), decay ** (length - i)
        for j in range(fields):
            straight = up * entering[0, j] + down * entering[1, j]
            coupled = up * entering[2, j] + down * entering[3, j]
            result[j, i] = base[j, i] + straight + celerity[i] * coupled
        copies.append(pltpu.make_async_copy(result.at[:, i], out.at[:, i], sems.at[i]))
        copies[-1].start()
    for copy in copies:
        copy.wait()


def finish(base, celerity, entering, decay):
    vmem = pl.BlockSpec(memory_space=pltpu.VMEM)
    return pl.pallas_call(
        functools.partial(finish_kernel, decay),
        out_shape=jax.ShapeDtypeStruct(base.shape, jnp.float32),
        in_specs=[vmem] * 3,
        out_specs=pl.BlockSpec(memory_space=pltpu.HBM),
        scratch_shapes=[
            pltpu.VMEM(base.shape, jnp.float32), pltpu.SemaphoreType.DMA((base.shape[1],))
        ],
        compiler_params=pltpu.CompilerParams(vmem_limit_bytes=24 * 2**20),
    )(base, celerity, entering)


def solution(mesh):
    count_x, count_y = mesh.shape["gx"], mesh.shape["gy"]

    def per_device(a, mass, level, m):
        decay, scale = line_constants(a.shape[1] * count_x)
        parts = exchange(a, mass, level, m, count_x, count_y, decay, scale)
        return finish(*parts, decay)

    in_specs = (P(None, "gx", "gy", "gz"), P("gx", "gy", "gz"), P("gx", "gy", "gz"), P())
    out_specs = P(None, "gx", "gy", "gz")
    return jax.shard_map(
        per_device, mesh=mesh, in_specs=in_specs, out_specs=out_specs, check_vma=False
    )
```

```python
import functools
import math

import jax
import jax.numpy as jnp
from jax import lax
from jax.experimental import pallas as pl
from jax.experimental.pallas import tpu as pltpu
from jax.sharding import PartitionSpec as P

MESH = pl.DeviceIdType.MESH
PIECES = 8
HALO = 8
STEPS = (4, 3, 5, 2, 6, 1, 7)


def line_constants(total_cells):
    stiffness = total_cells * total_cells / 4.0
    half = 1.0 + 0.5 / stiffness
    decay = half - math.sqrt(half**2 - 1.0)
    return decay, decay / (stiffness * (1.0 - decay * decay))


def remote(src, dst, send_sem, recv_sem, target):
    return pltpu.make_async_remote_copy(
        src_ref=src, dst_ref=dst, send_sem=send_sem, recv_sem=recv_sem,
        device_id=target, device_id_type=MESH,
    )


def edges(first, second):
    lane = lax.broadcasted_iota(jnp.int32, first.shape, first.ndim - 1)
    return jnp.where(lane < first.shape[-1] // 2, first, second)


def packed(first, second, low):
    row = lax.broadcasted_iota(jnp.int32, first.shape, first.ndim - 2)
    return jnp.where((row < 4) == low, first, pltpu.roll(second, 4, first.ndim - 2))


def slope(ext, edge, at_index, rows, lanes):
    at = lambda o: ext[(*at_index, slice(HALO + o, HALO + o + rows), slice(None))]
    ring = jnp.concatenate([at(0), edge[at_index]], axis=1)
    turn = lambda o: pltpu.roll(ring, (-o) % ring.shape[1], 1)[:, :lanes]
    return (
        0.75 * ((at(1) - at(-1)) + (turn(1) - turn(-1)))
        - 0.15 * ((at(2) - at(-2)) + (turn(2) - turn(-2)))
        + ((at(3) - at(-3)) + (turn(3) - turn(-3))) * (1.0 / 60.0)
    )


def exchange_kernel(
    count_x, count_y, decay, scale,
    a_ref, mass_ref, level_ref, m_ref, base, celerity, entering,
    a_v, mass, level, m, ends, own_in, own_out, pq, ext, u_edges, u_z, u_to_low, u_to_high,
    u_low, u_high, pq_ext, pq_edges, pq_z, p_low, p_high,
    load_sem, send1, recv1, send2, recv2, send_u, recv_u, send_p, recv_p,
):
    fields, length, rows, lanes = a_v.shape
    half = lanes // 2
    stride = count_x // PIECES
    my_x, my_y, my_z = (lax.axis_index(name) for name in ("gx", "gy", "gz"))
    has_low, has_high = my_y > 0, my_y < count_y - 1
    low, high, other = {"gy": my_y - 1}, {"gy": my_y + 1}, {"gz": 1 - my_z}

    load = pltpu.make_async_copy(a_ref, a_v, load_sem.at[0])
    load.start()
    later = [
        pltpu.make_async_copy(source, target, load_sem.at[1 + k])
        for k, (source, target) in enumerate(
            ((mass_ref, mass), (level_ref, level), (m_ref, m))
        )
    ]

    barrier = pltpu.get_barrier_semaphore()
    for step in range(1, count_x):
        peer = lax.rem(my_x + step, count_x)
        pl.semaphore_signal(barrier, inc=1, device_id={"gx": peer}, device_id_type=MESH)
    pl.semaphore_signal(barrier, inc=1, device_id=other, device_id_type=MESH)

    @pl.when(has_low)
    def _():
        for x in range(count_x):
            pl.semaphore_signal(
                barrier, inc=1, device_id={"gx": x, "gy": my_y - 1}, device_id_type=MESH
            )

    @pl.when(has_high)
    def _():
        for x in range(count_x):
            pl.semaphore_signal(
                barrier, inc=1, device_id={"gx": x, "gy": my_y + 1}, device_id_type=MESH
            )

    for copy in later:
        copy.start()

    load.wait()

    def field_ends(f, carry):
        upward = a_v[f, 0]
        downward = a_v[f, length - 1]
        for i in range(1, length):
            upward = a_v[f, i] + decay * upward
            downward = a_v[f, length - 1 - i] + decay * downward
        for yh in range(2):
            for kind in range(2):
                value = scale * (upward, downward)[kind][yh * 8 : yh * 8 + 8, :]
                for zh in range(2):
                    ends[yh * 4 + kind * 2 + zh, f] = value[:, zh * half : (zh + 1) * half]
        return carry

    lax.fori_loop(0, fields, field_ends, 0)

    neighbours = has_low.astype(jnp.int32) + has_high.astype(jnp.int32)
    pl.semaphore_wait(barrier, count_x * (1 + neighbours))

    my_piece = my_x // stride
    owner = lax.rem(my_x, stride) == 0
    steps = STEPS if stride == 1 else STEPS + (0,)

    def end_copy(step):
        piece = lax.rem(my_piece + step, PIECES)
        target = piece * stride
        return target, remote(
            ends.at[piece], own_in.at[my_x], send1.at[step], recv1.at[my_x], {"gx": target}
        )

    for step in steps:
        target, copy = end_copy(step)
        if stride == 1:
            copy.start()
        else:
            pl.when(target != my_x)(copy.start)
    if stride == 1:
        own_in[my_x] = ends[my_piece]
    else:

        @pl.when(owner)
        def _():
            own_in[my_x] = ends[my_piece]

    def field_solve(f, carry):
        upward = [a_v[f, 0]]
        for i in range(1, length):
            upward.append(a_v[f, i] + decay * upward[-1])
        down = jnp.zeros_like(upward[0])
        for i in range(length - 1, -1, -1):
            value = scale * (upward[i] + decay * down)
            down = a_v[f, i] + decay * down
            ext[f, i, HALO : HALO + rows, :] = value
            u_edges[f, i] = edges(value[:, :half], value[:, half:])
        for t in range(length // 2):
            u_to_low[f, t] = packed(
                ext[f, 2 * t, HALO : HALO + 8, :], ext[f, 2 * t + 1, HALO : HALO + 8, :], True
            )
            u_to_high[f, t] = packed(
                ext[f, 2 * t, HALO + rows - 8 : HALO + rows, :],
                ext[f, 2 * t + 1, HALO + rows - 8 : HALO + rows, :],
                False,
            )
        return carry

    lax.fori_loop(0, fields, field_solve, 0)
    copy_uz = remote(u_edges, u_z, send_u.at[0], recv_u.at[0], other)
    copy_uz.start()
    copy_ulow = remote(u_to_low, u_high, send_u.at[1], recv_u.at[1], low)
    copy_uhigh = remote(u_to_high, u_low, send_u.at[2], recv_u.at[2], high)
    pl.when(has_low)(copy_ulow.start)
    pl.when(has_high)(copy_uhigh.start)

    @pl.when(jnp.logical_not(has_low))
    def _():
        u_low[...] = jnp.zeros_like(u_low)
        p_low[...] = jnp.zeros_like(p_low)

    @pl.when(jnp.logical_not(has_high))
    def _():
        u_high[...] = jnp.zeros_like(u_high)
        p_high[...] = jnp.zeros_like(p_high)

    kind = lax.rem(my_piece // 2, 2)

    def result_copy(step):
        device = lax.rem(my_x + step, count_x)
        return remote(
            own_out.at[device], pq.at[my_piece], send2.at[step], recv2.at[my_piece],
            {"gx": device},
        )

    slot = lax.rem(my_piece, 4)
    to_low = jnp.logical_and(my_piece < 4, has_low)
    to_high = jnp.logical_and(my_piece >= 4, has_high)

    def low_copy(step):
        device = lax.rem(my_x + step, count_x)
        return remote(
            own_out.at[device], p_high.at[slot], send_p.at[1 + step], recv_p.at[5 + slot],
            {"gx": device, "gy": my_y - 1},
        )

    def high_copy(step):
        device = lax.rem(my_x + step, count_x)
        return remote(
            own_out.at[device], p_low.at[slot], send_p.at[1 + step], recv_p.at[1 + slot],
            {"gx": device, "gy": my_y + 1},
        )

    def own():
        for step in range(1, count_x):
            device = lax.rem(my_x + step, count_x)
            remote(
                own_in.at[device], own_in.at[device], send1.at[0], recv1.at[device],
                {"gx": device},
            ).wait_recv()

        def index(position):
            return jnp.where(kind == 1, count_x - 1 - position, position)

        power = decay**length
        total = own_in[index(0)]
        for position in range(1, count_x):
            total = own_in[index(position)] + power * total
        total = total * (1.0 / (1.0 - power**count_x))
        for position in range(count_x):
            device = index(position)
            own_out[device] = total
            if position < count_x - 1:
                total = own_in[device] + power * total
        for step in far_first:
            result_copy(step).start()

        @pl.when(to_low)
        def _():
            for step in far_first + [0]:
                low_copy(step).start()

        @pl.when(to_high)
        def _():
            for step in far_first + [0]:
                high_copy(step).start()

        pq[my_piece] = own_out[my_x]

    far_first = sorted(range(1, count_x), key=lambda step: abs(2 * step - count_x))
    if stride == 1:
        own()
    else:
        pl.when(owner)(own)

    copy_uz.wait_recv()
    pl.when(has_low)(copy_uhigh.wait_recv)
    pl.when(has_high)(copy_ulow.wait_recv)
    for copy in later:
        copy.wait()

    def field_halos(f, carry):
        for t in range(length // 2):
            ext[f, 2 * t, :HALO, :] = u_low[f, t]
            ext[f, 2 * t + 1, :HALO, :] = pltpu.roll(u_low[f, t], 4, 0)
            ext[f, 2 * t, HALO + rows :, :] = u_high[f, t]
            ext[f, 2 * t + 1, HALO + rows :, :] = pltpu.roll(u_high[f, t], 4, 0)
        return carry

    lax.fori_loop(0, fields, field_halos, 0)

    def couple(slopes, j):
        coupled = m[0, j] * slopes[0]
        for k in range(1, fields):
            coupled = coupled + m[k, j] * slopes[k]
        return coupled

    def plane(i, carry):
        speed = pressure_wave_celerity(mass[i], level[i])
        celerity[i] = speed
        slopes = [slope(ext, u_z, (f, i), rows, lanes) for f in range(fields)]
        for j in range(fields):
            base[j, i] = ext[j, i, HALO : HALO + rows, :] + speed * couple(slopes, j)
        return carry

    lax.fori_loop(0, length, plane, 0)

    for piece in range(PIECES):
        arrived = remote(
            own_out.at[0], pq.at[piece], send2.at[0], recv2.at[piece], {"gx": piece * stride}
        )
        pl.when(piece * stride != my_x)(arrived.wait_recv)

    for kd in range(2):
        for yh in range(2):
            piece = yh * 4 + kd * 2
            pq_edges[kd, :, yh * 8 : yh * 8 + 8, :] = edges(pq[piece], pq[piece + 1])
            for zh in range(2):
                pq_ext[
                    kd, :, HALO + yh * 8 : HALO + yh * 8 + 8, zh * half : (zh + 1) * half
                ] = pq[piece + zh]
    copy_pz = remote(pq_edges, pq_z, send_p.at[0], recv_p.at[0], other)
    copy_pz.start()
    entering[0:2] = pq_ext[:, :, HALO : HALO + rows, :]

    for step in steps:
        target, copy = end_copy(step)
        if stride == 1:
            copy.wait_send()
        else:
            pl.when(target != my_x)(copy.wait_send)
    copy_uz.wait_send()
    pl.when(has_low)(copy_ulow.wait_send)
    pl.when(has_high)(copy_uhigh.wait_send)

    def sent():
        for step in far_first:
            result_copy(step).wait_send()

        @pl.when(to_low)
        def _():
            for step in far_first + [0]:
                low_copy(step).wait_send()

        @pl.when(to_high)
        def _():
            for step in far_first + [0]:
                high_copy(step).wait_send()

    if stride == 1:
        sent()
    else:
        pl.when(owner)(sent)

    copy_pz.wait()

    @pl.when(has_low)
    def _():
        for k in range(4):
            remote(
                own_out.at[0], p_low.at[k], send_p.at[0], recv_p.at[1 + k],
                {"gx": (4 + k) * stride, "gy": my_y - 1},
            ).wait_recv()

    @pl.when(has_high)
    def _():
        for k in range(4):
            remote(
                own_out.at[0], p_high.at[k], send_p.at[0], recv_p.at[5 + k],
                {"gx": k * stride, "gy": my_y + 1},
            ).wait_recv()

    for zh in range(2):
        columns = slice(zh * half, (zh + 1) * half)
        for kd in range(2):
            pq_ext[kd, :, :HALO, columns] = p_low[2 * kd + zh]
            pq_ext[kd, :, HALO + rows :, columns] = p_high[2 * kd + zh]
    for kd in range(2):
        slopes = [slope(pq_ext, pq_z, (kd, f), rows, lanes) for f in range(fields)]
        for j in range(fields):
            entering[2 + kd, j] = couple(slopes, j)


def exchange(a, mass, level, m, count_x, count_y, decay, scale):
    fields, length, rows, lanes = a.shape
    half = lanes // 2
    vmem = pl.BlockSpec(memory_space=pltpu.VMEM)
    hbm = pl.BlockSpec(memory_space=pltpu.HBM)
    dma = pltpu.SemaphoreType.DMA
    buffer = lambda *sizes: pltpu.VMEM(sizes, jnp.float32)
    shape = lambda *sizes: jax.ShapeDtypeStruct(sizes, jnp.float32)
    return pl.pallas_call(
        functools.partial(exchange_kernel, count_x, count_y, decay, scale),
        out_shape=[
            shape(*a.shape), shape(length, rows, lanes), shape(4, fields, rows, lanes)
        ],
        in_specs=[hbm] * 4,
        out_specs=[vmem] * 3,
        scratch_shapes=[
            buffer(*a.shape), buffer(length, rows, lanes), buffer(length, rows, lanes),
            pltpu.SMEM((fields, fields), jnp.float32),
            buffer(PIECES, fields, 8, half),
            buffer(count_x, fields, 8, half),
            buffer(count_x, fields, 8, half),
            buffer(PIECES, fields, 8, half),
            buffer(fields, length, rows + 2 * HALO, lanes),
            buffer(fields, length, rows, half), buffer(fields, length, rows, half),
            buffer(fields, length // 2, 8, lanes), buffer(fields, length // 2, 8, lanes),
            buffer(fields, length // 2, 8, lanes), buffer(fields, length // 2, 8, lanes),
            buffer(2, fields, rows + 2 * HALO, lanes),
            buffer(2, fields, rows, half), buffer(2, fields, rows, half),
            buffer(4, fields, 8, half), buffer(4, fields, 8, half),
            dma((4,)), dma((PIECES,)), dma((count_x,)), dma((count_x,)), dma((PIECES,)),
            dma((3,)), dma((3,)), dma((count_x + 1,)), dma((9,)),
        ],
        compiler_params=pltpu.CompilerParams(
            collective_id=0, has_side_effects=True, vmem_limit_bytes=24 * 2**20
        ),
    )(*(pltpu.with_memory_space_constraint(x, pltpu.HBM) for x in (a, mass, level, m)))


def pressure_wave_celerity(mass, level):
    attraction = 1.5 * (1.0 + 0.392 * (1.0 - jnp.sqrt(level))) ** 2
    q = 1.0 + 0.5 * mass - 0.0625 * mass * mass
    return level / (1.0 - 0.25 * mass) ** 2 - attraction * (
        2.0 * mass * q - mass * mass * (0.5 - 0.125 * mass)
    ) / (q * q)


def finish_kernel(decay, base, celerity, entering, out, result, sems):
    fields, length, rows, lanes = base.shape
    copies = []
    for i in range(length):
        up, down = decay ** (i + 1), decay ** (length - i)
        for j in range(fields):
            straight = up * entering[0, j] + down * entering[1, j]
            coupled = up * entering[2, j] + down * entering[3, j]
            result[j, i] = base[j, i] + straight + celerity[i] * coupled
        copies.append(pltpu.make_async_copy(result.at[:, i], out.at[:, i], sems.at[i]))
        copies[-1].start()
    for copy in copies:
        copy.wait()


def finish(base, celerity, entering, decay):
    vmem = pl.BlockSpec(memory_space=pltpu.VMEM)
    return pl.pallas_call(
        functools.partial(finish_kernel, decay),
        out_shape=jax.ShapeDtypeStruct(base.shape, jnp.float32),
        in_specs=[vmem] * 3,
        out_specs=pl.BlockSpec(memory_space=pltpu.HBM),
        scratch_shapes=[
            pltpu.VMEM(base.shape, jnp.float32), pltpu.SemaphoreType.DMA((base.shape[1],))
        ],
        compiler_params=pltpu.CompilerParams(vmem_limit_bytes=24 * 2**20),
    )(base, celerity, entering)


def solution(mesh):
    count_x, count_y = mesh.shape["gx"], mesh.shape["gy"]

    def per_device(a, mass, level, m):
        decay, scale = line_constants(a.shape[1] * count_x)
        parts = exchange(a, mass, level, m, count_x, count_y, decay, scale)
        return finish(*parts, decay)

    in_specs = (P(None, "gx", "gy", "gz"), P("gx", "gy", "gz"), P("gx", "gy", "gz"), P())
    out_specs = P(None, "gx", "gy", "gz")
    return jax.shard_map(
        per_device, mesh=mesh, in_specs=in_specs, out_specs=out_specs, check_vma=False
    )
```

```python
import functools
import math

import jax
import jax.numpy as jnp
from jax import lax
from jax.experimental import pallas as pl
from jax.experimental.pallas import tpu as pltpu
from jax.sharding import PartitionSpec as P

MESH = pl.DeviceIdType.MESH
PIECES = 8
HALO = 8
STEPS = (4, 3, 5, 2, 6, 1, 7)


def line_constants(total_cells):
    stiffness = total_cells * total_cells / 4.0
    half = 1.0 + 0.5 / stiffness
    decay = half - math.sqrt(half**2 - 1.0)
    return decay, decay / (stiffness * (1.0 - decay * decay))


def remote(src, dst, send_sem, recv_sem, target):
    return pltpu.make_async_remote_copy(
        src_ref=src, dst_ref=dst, send_sem=send_sem, recv_sem=recv_sem,
        device_id=target, device_id_type=MESH,
    )


def edges(first, second):
    lane = lax.broadcasted_iota(jnp.int32, first.shape, first.ndim - 1)
    return jnp.where(lane < first.shape[-1] // 2, first, second)


def packed(first, second, low):
    row = lax.broadcasted_iota(jnp.int32, first.shape, first.ndim - 2)
    return jnp.where((row < 4) == low, first, pltpu.roll(second, 4, first.ndim - 2))


def slope(ext, edge, at_index, rows, lanes):
    at = lambda o: ext[(*at_index, slice(HALO + o, HALO + o + rows), slice(None))]
    ring = jnp.concatenate([at(0), edge[at_index]], axis=1)
    turn = lambda o: pltpu.roll(ring, (-o) % ring.shape[1], 1)[:, :lanes]
    return (
        0.75 * ((at(1) - at(-1)) + (turn(1) - turn(-1)))
        - 0.15 * ((at(2) - at(-2)) + (turn(2) - turn(-2)))
        + ((at(3) - at(-3)) + (turn(3) - turn(-3))) * (1.0 / 60.0)
    )


def exchange_kernel(
    count_x, count_y, decay, scale,
    a_ref, mass_ref, level_ref, m_ref, base, celerity, entering,
    a_v, mass, level, m, ends, own_in, own_out, own_halo, pq, ext, u_edges, u_z, u_to_low, u_to_high,
    u_low, u_high, pq_ext, pq_edges, pq_z, p_low, p_high,
    load_sem, send1, recv1, send2, recv2, send_u, recv_u, send_p, recv_p,
):
    fields, length, rows, lanes = a_v.shape
    half = lanes // 2
    stride = count_x // PIECES
    my_x, my_y, my_z = (lax.axis_index(name) for name in ("gx", "gy", "gz"))
    has_low, has_high = my_y > 0, my_y < count_y - 1
    low, high, other = {"gy": my_y - 1}, {"gy": my_y + 1}, {"gz": 1 - my_z}

    load = pltpu.make_async_copy(a_ref, a_v, load_sem.at[0])
    load.start()
    later = [
        pltpu.make_async_copy(source, target, load_sem.at[1 + k])
        for k, (source, target) in enumerate(
            ((mass_ref, mass), (level_ref, level), (m_ref, m))
        )
    ]

    barrier = pltpu.get_barrier_semaphore()
    for step in range(1, count_x):
        peer = lax.rem(my_x + step, count_x)
        pl.semaphore_signal(barrier, inc=1, device_id={"gx": peer}, device_id_type=MESH)
    pl.semaphore_signal(barrier, inc=1, device_id=other, device_id_type=MESH)

    @pl.when(has_low)
    def _():
        for x in range(count_x):
            pl.semaphore_signal(
                barrier, inc=1, device_id={"gx": x, "gy": my_y - 1}, device_id_type=MESH
            )

    @pl.when(has_high)
    def _():
        for x in range(count_x):
            pl.semaphore_signal(
                barrier, inc=1, device_id={"gx": x, "gy": my_y + 1}, device_id_type=MESH
            )

    for copy in later:
        copy.start()

    load.wait()

    def field_ends(f, carry):
        upward = a_v[f, 0]
        downward = a_v[f, length - 1]
        for i in range(1, length):
            upward = a_v[f, i] + decay * upward
            downward = a_v[f, length - 1 - i] + decay * downward
        for yh in range(2):
            for kind in range(2):
                value = scale * (upward, downward)[kind][yh * 8 : yh * 8 + 8, :]
                for zh in range(2):
                    ends[yh * 4 + kind * 2 + zh, f] = value[:, zh * half : (zh + 1) * half]
        return carry

    lax.fori_loop(0, fields, field_ends, 0)

    neighbours = has_low.astype(jnp.int32) + has_high.astype(jnp.int32)
    pl.semaphore_wait(barrier, count_x * (1 + neighbours))

    my_piece = my_x // stride
    owner = lax.rem(my_x, stride) == 0
    steps = STEPS if stride == 1 else STEPS + (0,)

    def end_copy(step):
        piece = lax.rem(my_piece + step, PIECES)
        target = piece * stride
        return target, remote(
            ends.at[piece], own_in.at[my_x], send1.at[step], recv1.at[my_x], {"gx": target}
        )

    for step in steps:
        target, copy = end_copy(step)
        if stride == 1:
            copy.start()
        else:
            pl.when(target != my_x)(copy.start)
    if stride == 1:
        own_in[my_x] = ends[my_piece]
    else:

        @pl.when(owner)
        def _():
            own_in[my_x] = ends[my_piece]

    def field_solve(f, carry):
        upward = [a_v[f, 0]]
        for i in range(1, length):
            upward.append(a_v[f, i] + decay * upward[-1])
        down = jnp.zeros_like(upward[0])
        for i in range(length - 1, -1, -1):
            value = scale * (upward[i] + decay * down)
            down = a_v[f, i] + decay * down
            ext[f, i, HALO : HALO + rows, :] = value
            u_edges[f, i] = edges(value[:, :half], value[:, half:])
        for t in range(length // 2):
            u_to_low[f, t] = packed(
                ext[f, 2 * t, HALO : HALO + 8, :], ext[f, 2 * t + 1, HALO : HALO + 8, :], True
            )
            u_to_high[f, t] = packed(
                ext[f, 2 * t, HALO + rows - 8 : HALO + rows, :],
                ext[f, 2 * t + 1, HALO + rows - 8 : HALO + rows, :],
                False,
            )
        return carry

    lax.fori_loop(0, fields, field_solve, 0)
    copy_uz = remote(u_edges, u_z, send_u.at[0], recv_u.at[0], other)
    copy_uz.start()
    copy_ulow = remote(u_to_low, u_high, send_u.at[1], recv_u.at[1], low)
    copy_uhigh = remote(u_to_high, u_low, send_u.at[2], recv_u.at[2], high)
    pl.when(has_low)(copy_ulow.start)
    pl.when(has_high)(copy_uhigh.start)

    @pl.when(jnp.logical_not(has_low))
    def _():
        u_low[...] = jnp.zeros_like(u_low)
        p_low[...] = jnp.zeros_like(p_low)

    @pl.when(jnp.logical_not(has_high))
    def _():
        u_high[...] = jnp.zeros_like(u_high)
        p_high[...] = jnp.zeros_like(p_high)

    kind = lax.rem(my_piece // 2, 2)

    def result_copy(step):
        device = lax.rem(my_x + step, count_x)
        return remote(
            own_out.at[device], pq.at[my_piece], send2.at[step], recv2.at[my_piece],
            {"gx": device},
        )

    slot = lax.rem(my_piece, 4)
    to_low = jnp.logical_and(my_piece < 4, has_low)
    to_high = jnp.logical_and(my_piece >= 4, has_high)

    def pack_halo(is_low):
        for t in range(fields // 2):
            own_halo[:, t] = packed(own_out[:, 2 * t], own_out[:, 2 * t + 1], is_low)
        if fields % 2:
            own_halo[:, fields // 2] = own_out[:, fields - 1]

    def low_copy(step):
        device = lax.rem(my_x + step, count_x)
        return remote(
            own_halo.at[device], p_high.at[slot], send_p.at[1 + step], recv_p.at[5 + slot],
            {"gx": device, "gy": my_y - 1},
        )

    def high_copy(step):
        device = lax.rem(my_x + step, count_x)
        return remote(
            own_halo.at[device], p_low.at[slot], send_p.at[1 + step], recv_p.at[1 + slot],
            {"gx": device, "gy": my_y + 1},
        )

    def own():
        for step in range(1, count_x):
            device = lax.rem(my_x + step, count_x)
            remote(
                own_in.at[device], own_in.at[device], send1.at[0], recv1.at[device],
                {"gx": device},
            ).wait_recv()

        def index(position):
            return jnp.where(kind == 1, count_x - 1 - position, position)

        power = decay**length
        total = own_in[index(0)]
        for position in range(1, count_x):
            total = own_in[index(position)] + power * total
        total = total * (1.0 / (1.0 - power**count_x))
        for position in range(count_x):
            device = index(position)
            own_out[device] = total
            if position < count_x - 1:
                total = own_in[device] + power * total
        for step in far_first:
            result_copy(step).start()

        @pl.when(to_low)
        def _():
            pack_halo(True)
            for step in far_first + [0]:
                low_copy(step).start()

        @pl.when(to_high)
        def _():
            pack_halo(False)
            for step in far_first + [0]:
                high_copy(step).start()

        pq[my_piece] = own_out[my_x]

    far_first = sorted(range(1, count_x), key=lambda step: abs(2 * step - count_x))
    if stride == 1:
        own()
    else:
        pl.when(owner)(own)

    copy_uz.wait_recv()
    pl.when(has_low)(copy_uhigh.wait_recv)
    pl.when(has_high)(copy_ulow.wait_recv)
    for copy in later:
        copy.wait()

    def field_halos(f, carry):
        for t in range(length // 2):
            ext[f, 2 * t, :HALO, :] = u_low[f, t]
            ext[f, 2 * t + 1, :HALO, :] = pltpu.roll(u_low[f, t], 4, 0)
            ext[f, 2 * t, HALO + rows :, :] = u_high[f, t]
            ext[f, 2 * t + 1, HALO + rows :, :] = pltpu.roll(u_high[f, t], 4, 0)
        return carry

    lax.fori_loop(0, fields, field_halos, 0)

    def couple(slopes, j):
        coupled = m[0, j] * slopes[0]
        for k in range(1, fields):
            coupled = coupled + m[k, j] * slopes[k]
        return coupled

    def plane(i, carry):
        speed = pressure_wave_celerity(mass[i], level[i])
        celerity[i] = speed
        slopes = [slope(ext, u_z, (f, i), rows, lanes) for f in range(fields)]
        for j in range(fields):
            base[j, i] = ext[j, i, HALO : HALO + rows, :] + speed * couple(slopes, j)
        return carry

    lax.fori_loop(0, length, plane, 0)

    for piece in range(PIECES):
        arrived = remote(
            own_out.at[0], pq.at[piece], send2.at[0], recv2.at[piece], {"gx": piece * stride}
        )
        pl.when(piece * stride != my_x)(arrived.wait_recv)

    for kd in range(2):
        for yh in range(2):
            piece = yh * 4 + kd * 2
            pq_edges[kd, :, yh * 8 : yh * 8 + 8, :] = edges(pq[piece], pq[piece + 1])
            for zh in range(2):
                pq_ext[
                    kd, :, HALO + yh * 8 : HALO + yh * 8 + 8, zh * half : (zh + 1) * half
                ] = pq[piece + zh]
    copy_pz = remote(pq_edges, pq_z, send_p.at[0], recv_p.at[0], other)
    copy_pz.start()
    entering[0:2] = pq_ext[:, :, HALO : HALO + rows, :]

    for step in steps:
        target, copy = end_copy(step)
        if stride == 1:
            copy.wait_send()
        else:
            pl.when(target != my_x)(copy.wait_send)
    copy_uz.wait_send()
    pl.when(has_low)(copy_ulow.wait_send)
    pl.when(has_high)(copy_uhigh.wait_send)

    def sent():
        for step in far_first:
            result_copy(step).wait_send()

        @pl.when(to_low)
        def _():
            for step in far_first + [0]:
                low_copy(step).wait_send()

        @pl.when(to_high)
        def _():
            for step in far_first + [0]:
                high_copy(step).wait_send()

    if stride == 1:
        sent()
    else:
        pl.when(owner)(sent)

    copy_pz.wait()

    @pl.when(has_low)
    def _():
        for k in range(4):
            remote(
                own_halo.at[0], p_low.at[k], send_p.at[0], recv_p.at[1 + k],
                {"gx": (4 + k) * stride, "gy": my_y - 1},
            ).wait_recv()

    @pl.when(has_high)
    def _():
        for k in range(4):
            remote(
                own_halo.at[0], p_high.at[k], send_p.at[0], recv_p.at[5 + k],
                {"gx": k * stride, "gy": my_y + 1},
            ).wait_recv()

    for zh in range(2):
        columns = slice(zh * half, (zh + 1) * half)
        for kd in range(2):
            for f in range(fields):
                below, above = p_low[2 * kd + zh, f // 2], p_high[2 * kd + zh, f // 2]
                if f % 2:
                    below, above = pltpu.roll(below, 4, 0), pltpu.roll(above, 4, 0)
                pq_ext[kd, f, :HALO, columns] = below
                pq_ext[kd, f, HALO + rows :, columns] = above
    for kd in range(2):
        slopes = [slope(pq_ext, pq_z, (kd, f), rows, lanes) for f in range(fields)]
        for j in range(fields):
            entering[2 + kd, j] = couple(slopes, j)


def exchange(a, mass, level, m, count_x, count_y, decay, scale):
    fields, length, rows, lanes = a.shape
    half = lanes // 2
    vmem = pl.BlockSpec(memory_space=pltpu.VMEM)
    hbm = pl.BlockSpec(memory_space=pltpu.HBM)
    dma = pltpu.SemaphoreType.DMA
    buffer = lambda *sizes: pltpu.VMEM(sizes, jnp.float32)
    shape = lambda *sizes: jax.ShapeDtypeStruct(sizes, jnp.float32)
    return pl.pallas_call(
        functools.partial(exchange_kernel, count_x, count_y, decay, scale),
        out_shape=[
            shape(*a.shape), shape(length, rows, lanes), shape(4, fields, rows, lanes)
        ],
        in_specs=[hbm] * 4,
        out_specs=[vmem] * 3,
        scratch_shapes=[
            buffer(*a.shape), buffer(length, rows, lanes), buffer(length, rows, lanes),
            pltpu.SMEM((fields, fields), jnp.float32),
            buffer(PIECES, fields, 8, half),
            buffer(count_x, fields, 8, half),
            buffer(count_x, fields, 8, half),
            buffer(count_x, (fields + 1) // 2, 8, half),
            buffer(PIECES, fields, 8, half),
            buffer(fields, length, rows + 2 * HALO, lanes),
            buffer(fields, length, rows, half), buffer(fields, length, rows, half),
            buffer(fields, length // 2, 8, lanes), buffer(fields, length // 2, 8, lanes),
            buffer(fields, length // 2, 8, lanes), buffer(fields, length // 2, 8, lanes),
            buffer(2, fields, rows + 2 * HALO, lanes),
            buffer(2, fields, rows, half), buffer(2, fields, rows, half),
            buffer(4, (fields + 1) // 2, 8, half), buffer(4, (fields + 1) // 2, 8, half),
            dma((4,)), dma((PIECES,)), dma((count_x,)), dma((count_x,)), dma((PIECES,)),
            dma((3,)), dma((3,)), dma((count_x + 1,)), dma((9,)),
        ],
        compiler_params=pltpu.CompilerParams(
            collective_id=0, has_side_effects=True, vmem_limit_bytes=24 * 2**20
        ),
    )(*(pltpu.with_memory_space_constraint(x, pltpu.HBM) for x in (a, mass, level, m)))


def pressure_wave_celerity(mass, level):
    attraction = 1.5 * (1.0 + 0.392 * (1.0 - jnp.sqrt(level))) ** 2
    q = 1.0 + 0.5 * mass - 0.0625 * mass * mass
    return level / (1.0 - 0.25 * mass) ** 2 - attraction * (
        2.0 * mass * q - mass * mass * (0.5 - 0.125 * mass)
    ) / (q * q)


def finish_kernel(decay, base, celerity, entering, out, result, sems):
    fields, length, rows, lanes = base.shape
    copies = []
    for i in range(length):
        up, down = decay ** (i + 1), decay ** (length - i)
        for j in range(fields):
            straight = up * entering[0, j] + down * entering[1, j]
            coupled = up * entering[2, j] + down * entering[3, j]
            result[j, i] = base[j, i] + straight + celerity[i] * coupled
        copies.append(pltpu.make_async_copy(result.at[:, i], out.at[:, i], sems.at[i]))
        copies[-1].start()
    for copy in copies:
        copy.wait()


def finish(base, celerity, entering, decay):
    vmem = pl.BlockSpec(memory_space=pltpu.VMEM)
    return pl.pallas_call(
        functools.partial(finish_kernel, decay),
        out_shape=jax.ShapeDtypeStruct(base.shape, jnp.float32),
        in_specs=[vmem] * 3,
        out_specs=pl.BlockSpec(memory_space=pltpu.HBM),
        scratch_shapes=[
            pltpu.VMEM(base.shape, jnp.float32), pltpu.SemaphoreType.DMA((base.shape[1],))
        ],
        compiler_params=pltpu.CompilerParams(vmem_limit_bytes=24 * 2**20),
    )(base, celerity, entering)


def solution(mesh):
    count_x, count_y = mesh.shape["gx"], mesh.shape["gy"]

    def per_device(a, mass, level, m):
        decay, scale = line_constants(a.shape[1] * count_x)
        parts = exchange(a, mass, level, m, count_x, count_y, decay, scale)
        return finish(*parts, decay)

    in_specs = (P(None, "gx", "gy", "gz"), P("gx", "gy", "gz"), P("gx", "gy", "gz"), P())
    out_specs = P(None, "gx", "gy", "gz")
    return jax.shard_map(
        per_device, mesh=mesh, in_specs=in_specs, out_specs=out_specs, check_vma=False
    )
```

```python
import functools
import math

import jax
import jax.numpy as jnp
from jax import lax
from jax.experimental import pallas as pl
from jax.experimental.pallas import tpu as pltpu
from jax.sharding import PartitionSpec as P

MESH = pl.DeviceIdType.MESH
PIECES = 8
HALO = 8
STEPS = (4, 3, 5, 2, 6, 1, 7)


def line_constants(total_cells):
    stiffness = total_cells * total_cells / 4.0
    half = 1.0 + 0.5 / stiffness
    decay = half - math.sqrt(half**2 - 1.0)
    return decay, decay / (stiffness * (1.0 - decay * decay))


def remote(src, dst, send_sem, recv_sem, target):
    return pltpu.make_async_remote_copy(
        src_ref=src, dst_ref=dst, send_sem=send_sem, recv_sem=recv_sem,
        device_id=target, device_id_type=MESH,
    )


def edges(first, second):
    lane = lax.broadcasted_iota(jnp.int32, first.shape, first.ndim - 1)
    return jnp.where(lane < first.shape[-1] // 2, first, second)


def packed(first, second, low):
    row = lax.broadcasted_iota(jnp.int32, first.shape, first.ndim - 2)
    return jnp.where((row < 4) == low, first, pltpu.roll(second, 4, first.ndim - 2))


def slope(ext, edge, at_index, rows, lanes):
    at = lambda o: ext[(*at_index, slice(HALO + o, HALO + o + rows), slice(None))]
    ring = jnp.concatenate([at(0), edge[at_index]], axis=1)
    turn = lambda o: pltpu.roll(ring, (-o) % ring.shape[1], 1)[:, :lanes]
    return (
        0.75 * ((at(1) - at(-1)) + (turn(1) - turn(-1)))
        - 0.15 * ((at(2) - at(-2)) + (turn(2) - turn(-2)))
        + ((at(3) - at(-3)) + (turn(3) - turn(-3))) * (1.0 / 60.0)
    )


def exchange_kernel(
    count_x, count_y, decay, scale,
    a_ref, mass_ref, level_ref, m_ref, base, celerity, entering,
    a_v, mass, level, m, ends, own_in, own_out, own_halo, pq, ext, u_edges, u_z, u_to_low, u_to_high,
    u_low, u_high, pq_ext, pq_edges, pq_z, p_low, p_high,
    load_sem, send1, recv1, send2, recv2, send_u, recv_u, send_p, recv_p, send_z, recv_z,
):
    fields, length, rows, lanes = a_v.shape
    half = lanes // 2
    stride = count_x // PIECES
    my_x, my_y, my_z = (lax.axis_index(name) for name in ("gx", "gy", "gz"))
    has_low, has_high = my_y > 0, my_y < count_y - 1
    low, high, other = {"gy": my_y - 1}, {"gy": my_y + 1}, {"gz": 1 - my_z}

    load = pltpu.make_async_copy(a_ref, a_v, load_sem.at[0])
    load.start()
    later = [
        pltpu.make_async_copy(source, target, load_sem.at[1 + k])
        for k, (source, target) in enumerate(
            ((mass_ref, mass), (level_ref, level), (m_ref, m))
        )
    ]

    barrier = pltpu.get_barrier_semaphore()
    for step in range(1, count_x):
        peer = lax.rem(my_x + step, count_x)
        pl.semaphore_signal(barrier, inc=1, device_id={"gx": peer}, device_id_type=MESH)
    pl.semaphore_signal(barrier, inc=1, device_id=other, device_id_type=MESH)

    @pl.when(has_low)
    def _():
        for x in range(count_x):
            pl.semaphore_signal(
                barrier, inc=1, device_id={"gx": x, "gy": my_y - 1}, device_id_type=MESH
            )

    @pl.when(has_high)
    def _():
        for x in range(count_x):
            pl.semaphore_signal(
                barrier, inc=1, device_id={"gx": x, "gy": my_y + 1}, device_id_type=MESH
            )

    for copy in later:
        copy.start()

    load.wait()

    def field_ends(f, carry):
        upward = a_v[f, 0]
        downward = a_v[f, length - 1]
        for i in range(1, length):
            upward = a_v[f, i] + decay * upward
            downward = a_v[f, length - 1 - i] + decay * downward
        for yh in range(2):
            for kind in range(2):
                value = scale * (upward, downward)[kind][yh * 8 : yh * 8 + 8, :]
                for zh in range(2):
                    ends[yh * 4 + kind * 2 + zh, f] = value[:, zh * half : (zh + 1) * half]
        return carry

    lax.fori_loop(0, fields, field_ends, 0)

    neighbours = has_low.astype(jnp.int32) + has_high.astype(jnp.int32)
    pl.semaphore_wait(barrier, count_x * (1 + neighbours))

    my_piece = my_x // stride
    owner = lax.rem(my_x, stride) == 0
    steps = STEPS if stride == 1 else STEPS + (0,)

    def end_copy(step):
        piece = lax.rem(my_piece + step, PIECES)
        target = piece * stride
        return target, remote(
            ends.at[piece], own_in.at[my_x], send1.at[step], recv1.at[my_x], {"gx": target}
        )

    for step in steps:
        target, copy = end_copy(step)
        if stride == 1:
            copy.start()
        else:
            pl.when(target != my_x)(copy.start)
    if stride == 1:
        own_in[my_x] = ends[my_piece]
    else:

        @pl.when(owner)
        def _():
            own_in[my_x] = ends[my_piece]

    def field_solve(f, carry):
        upward = [a_v[f, 0]]
        for i in range(1, length):
            upward.append(a_v[f, i] + decay * upward[-1])
        down = jnp.zeros_like(upward[0])
        for i in range(length - 1, -1, -1):
            value = scale * (upward[i] + decay * down)
            down = a_v[f, i] + decay * down
            ext[f, i, HALO : HALO + rows, :] = value
            u_edges[f, i] = edges(value[:, :half], value[:, half:])
        for t in range(length // 2):
            u_to_low[f, t] = packed(
                ext[f, 2 * t, HALO : HALO + 8, :], ext[f, 2 * t + 1, HALO : HALO + 8, :], True
            )
            u_to_high[f, t] = packed(
                ext[f, 2 * t, HALO + rows - 8 : HALO + rows, :],
                ext[f, 2 * t + 1, HALO + rows - 8 : HALO + rows, :],
                False,
            )
        return carry

    lax.fori_loop(0, fields, field_solve, 0)
    copy_uz = remote(u_edges, u_z, send_u.at[0], recv_u.at[0], other)
    copy_uz.start()
    copy_ulow = remote(u_to_low, u_high, send_u.at[1], recv_u.at[1], low)
    copy_uhigh = remote(u_to_high, u_low, send_u.at[2], recv_u.at[2], high)
    pl.when(has_low)(copy_ulow.start)
    pl.when(has_high)(copy_uhigh.start)

    @pl.when(jnp.logical_not(has_low))
    def _():
        u_low[...] = jnp.zeros_like(u_low)
        p_low[...] = jnp.zeros_like(p_low)

    @pl.when(jnp.logical_not(has_high))
    def _():
        u_high[...] = jnp.zeros_like(u_high)
        p_high[...] = jnp.zeros_like(p_high)

    kind = lax.rem(my_piece // 2, 2)

    def result_copy(step):
        device = lax.rem(my_x + step, count_x)
        return remote(
            own_out.at[device], pq.at[my_piece], send2.at[step], recv2.at[my_piece],
            {"gx": device},
        )

    slot = lax.rem(my_piece, 4)
    to_low = jnp.logical_and(my_piece < 4, has_low)
    to_high = jnp.logical_and(my_piece >= 4, has_high)

    def pack_halo(is_low):
        for t in range(fields // 2):
            own_halo[:, t] = packed(own_out[:, 2 * t], own_out[:, 2 * t + 1], is_low)
        if fields % 2:
            own_halo[:, fields // 2] = own_out[:, fields - 1]

    def low_copy(step):
        device = lax.rem(my_x + step, count_x)
        return remote(
            own_halo.at[device], p_high.at[slot], send_p.at[1 + step], recv_p.at[5 + slot],
            {"gx": device, "gy": my_y - 1},
        )

    def high_copy(step):
        device = lax.rem(my_x + step, count_x)
        return remote(
            own_halo.at[device], p_low.at[slot], send_p.at[1 + step], recv_p.at[1 + slot],
            {"gx": device, "gy": my_y + 1},
        )

    def own():
        for step in range(1, count_x):
            device = lax.rem(my_x + step, count_x)
            remote(
                own_in.at[device], own_in.at[device], send1.at[0], recv1.at[device],
                {"gx": device},
            ).wait_recv()

        def index(position):
            return jnp.where(kind == 1, count_x - 1 - position, position)

        power = decay**length
        total = own_in[index(0)]
        for position in range(1, count_x):
            total = own_in[index(position)] + power * total
        total = total * (1.0 / (1.0 - power**count_x))
        for position in range(count_x):
            device = index(position)
            own_out[device] = total
            if position < count_x - 1:
                total = own_in[device] + power * total
        for step in far_first:
            result_copy(step).start()

        @pl.when(to_low)
        def _():
            pack_halo(True)
            for step in far_first + [0]:
                low_copy(step).start()

        @pl.when(to_high)
        def _():
            pack_halo(False)
            for step in far_first + [0]:
                high_copy(step).start()

        pq[my_piece] = own_out[my_x]

    far_first = sorted(range(1, count_x), key=lambda step: abs(2 * step - count_x))
    if stride == 1:
        own()
    else:
        pl.when(owner)(own)

    copy_uz.wait_recv()
    pl.when(has_low)(copy_uhigh.wait_recv)
    pl.when(has_high)(copy_ulow.wait_recv)
    for copy in later:
        copy.wait()

    def field_halos(f, carry):
        for t in range(length // 2):
            ext[f, 2 * t, :HALO, :] = u_low[f, t]
            ext[f, 2 * t + 1, :HALO, :] = pltpu.roll(u_low[f, t], 4, 0)
            ext[f, 2 * t, HALO + rows :, :] = u_high[f, t]
            ext[f, 2 * t + 1, HALO + rows :, :] = pltpu.roll(u_high[f, t], 4, 0)
        return carry

    lax.fori_loop(0, fields, field_halos, 0)

    def couple(slopes, j):
        coupled = m[0, j] * slopes[0]
        for k in range(1, fields):
            coupled = coupled + m[k, j] * slopes[k]
        return coupled

    def plane(i, carry):
        speed = pressure_wave_celerity(mass[i], level[i])
        celerity[i] = speed
        slopes = [slope(ext, u_z, (f, i), rows, lanes) for f in range(fields)]
        for j in range(fields):
            base[j, i] = ext[j, i, HALO : HALO + rows, :] + speed * couple(slopes, j)
        return carry

    lax.fori_loop(0, length, plane, 0)

    last = []
    for yh in range(2):
        for kd in range(2):
            first = yh * 4 + kd * 2
            at = slice(yh * 8, yh * 8 + 8)
            for piece in (first, first + 1):
                arrived = remote(
                    own_out.at[0], pq.at[piece], send2.at[0], recv2.at[piece],
                    {"gx": piece * stride},
                )
                pl.when(piece * stride != my_x)(arrived.wait_recv)
            pq_edges[kd, :, at, :] = edges(pq[first], pq[first + 1])
            last.append(
                remote(
                    pq_edges.at[kd, :, at, :], pq_z.at[kd, :, at, :],
                    send_z.at[yh * 2 + kd], recv_z.at[yh * 2 + kd], other,
                )
            )
            last[-1].start()
            for zh in range(2):
                pq_ext[
                    kd, :, HALO + yh * 8 : HALO + yh * 8 + 8, zh * half : (zh + 1) * half
                ] = pq[first + zh]
    entering[0:2] = pq_ext[:, :, HALO : HALO + rows, :]

    for step in steps:
        target, copy = end_copy(step)
        if stride == 1:
            copy.wait_send()
        else:
            pl.when(target != my_x)(copy.wait_send)
    copy_uz.wait_send()
    pl.when(has_low)(copy_ulow.wait_send)
    pl.when(has_high)(copy_uhigh.wait_send)

    def sent():
        for step in far_first:
            result_copy(step).wait_send()

        @pl.when(to_low)
        def _():
            for step in far_first + [0]:
                low_copy(step).wait_send()

        @pl.when(to_high)
        def _():
            for step in far_first + [0]:
                high_copy(step).wait_send()

    if stride == 1:
        sent()
    else:
        pl.when(owner)(sent)

    for copy in last:
        copy.wait()

    @pl.when(has_low)
    def _():
        for k in range(4):
            remote(
                own_halo.at[0], p_low.at[k], send_p.at[0], recv_p.at[1 + k],
                {"gx": (4 + k) * stride, "gy": my_y - 1},
            ).wait_recv()

    @pl.when(has_high)
    def _():
        for k in range(4):
            remote(
                own_halo.at[0], p_high.at[k], send_p.at[0], recv_p.at[5 + k],
                {"gx": k * stride, "gy": my_y + 1},
            ).wait_recv()

    for zh in range(2):
        columns = slice(zh * half, (zh + 1) * half)
        for kd in range(2):
            for f in range(fields):
                below, above = p_low[2 * kd + zh, f // 2], p_high[2 * kd + zh, f // 2]
                if f % 2:
                    below, above = pltpu.roll(below, 4, 0), pltpu.roll(above, 4, 0)
                pq_ext[kd, f, :HALO, columns] = below
                pq_ext[kd, f, HALO + rows :, columns] = above
    for kd in range(2):
        slopes = [slope(pq_ext, pq_z, (kd, f), rows, lanes) for f in range(fields)]
        for j in range(fields):
            entering[2 + kd, j] = couple(slopes, j)


def exchange(a, mass, level, m, count_x, count_y, decay, scale):
    fields, length, rows, lanes = a.shape
    half = lanes // 2
    vmem = pl.BlockSpec(memory_space=pltpu.VMEM)
    hbm = pl.BlockSpec(memory_space=pltpu.HBM)
    dma = pltpu.SemaphoreType.DMA
    buffer = lambda *sizes: pltpu.VMEM(sizes, jnp.float32)
    shape = lambda *sizes: jax.ShapeDtypeStruct(sizes, jnp.float32)
    return pl.pallas_call(
        functools.partial(exchange_kernel, count_x, count_y, decay, scale),
        out_shape=[
            shape(*a.shape), shape(length, rows, lanes), shape(4, fields, rows, lanes)
        ],
        in_specs=[hbm] * 4,
        out_specs=[vmem] * 3,
        scratch_shapes=[
            buffer(*a.shape), buffer(length, rows, lanes), buffer(length, rows, lanes),
            pltpu.SMEM((fields, fields), jnp.float32),
            buffer(PIECES, fields, 8, half),
            buffer(count_x, fields, 8, half),
            buffer(count_x, fields, 8, half),
            buffer(count_x, (fields + 1) // 2, 8, half),
            buffer(PIECES, fields, 8, half),
            buffer(fields, length, rows + 2 * HALO, lanes),
            buffer(fields, length, rows, half), buffer(fields, length, rows, half),
            buffer(fields, length // 2, 8, lanes), buffer(fields, length // 2, 8, lanes),
            buffer(fields, length // 2, 8, lanes), buffer(fields, length // 2, 8, lanes),
            buffer(2, fields, rows + 2 * HALO, lanes),
            buffer(2, fields, rows, half), buffer(2, fields, rows, half),
            buffer(4, (fields + 1) // 2, 8, half), buffer(4, (fields + 1) // 2, 8, half),
            dma((4,)), dma((PIECES,)), dma((count_x,)), dma((count_x,)), dma((PIECES,)),
            dma((3,)), dma((3,)), dma((count_x + 1,)), dma((9,)),
            dma((4,)), dma((4,)),
        ],
        compiler_params=pltpu.CompilerParams(
            collective_id=0, has_side_effects=True, vmem_limit_bytes=24 * 2**20
        ),
    )(*(pltpu.with_memory_space_constraint(x, pltpu.HBM) for x in (a, mass, level, m)))


def pressure_wave_celerity(mass, level):
    attraction = 1.5 * (1.0 + 0.392 * (1.0 - jnp.sqrt(level))) ** 2
    q = 1.0 + 0.5 * mass - 0.0625 * mass * mass
    return level / (1.0 - 0.25 * mass) ** 2 - attraction * (
        2.0 * mass * q - mass * mass * (0.5 - 0.125 * mass)
    ) / (q * q)


def finish_kernel(decay, base, celerity, entering, out, result, sems):
    fields, length, rows, lanes = base.shape
    copies = []
    for i in range(length):
        up, down = decay ** (i + 1), decay ** (length - i)
        for j in range(fields):
            straight = up * entering[0, j] + down * entering[1, j]
            coupled = up * entering[2, j] + down * entering[3, j]
            result[j, i] = base[j, i] + straight + celerity[i] * coupled
        copies.append(pltpu.make_async_copy(result.at[:, i], out.at[:, i], sems.at[i]))
        copies[-1].start()
    for copy in copies:
        copy.wait()


def finish(base, celerity, entering, decay):
    vmem = pl.BlockSpec(memory_space=pltpu.VMEM)
    return pl.pallas_call(
        functools.partial(finish_kernel, decay),
        out_shape=jax.ShapeDtypeStruct(base.shape, jnp.float32),
        in_specs=[vmem] * 3,
        out_specs=pl.BlockSpec(memory_space=pltpu.HBM),
        scratch_shapes=[
            pltpu.VMEM(base.shape, jnp.float32), pltpu.SemaphoreType.DMA((base.shape[1],))
        ],
        compiler_params=pltpu.CompilerParams(vmem_limit_bytes=24 * 2**20),
    )(base, celerity, entering)


def solution(mesh):
    count_x, count_y = mesh.shape["gx"], mesh.shape["gy"]

    def per_device(a, mass, level, m):
        decay, scale = line_constants(a.shape[1] * count_x)
        parts = exchange(a, mass, level, m, count_x, count_y, decay, scale)
        return finish(*parts, decay)

    in_specs = (P(None, "gx", "gy", "gz"), P("gx", "gy", "gz"), P("gx", "gy", "gz"), P())
    out_specs = P(None, "gx", "gy", "gz")
    return jax.shard_map(
        per_device, mesh=mesh, in_specs=in_specs, out_specs=out_specs, check_vma=False
    )
```
